256 devices in a mesh: ctx: 32 (over y, z), tp: 8 (over x, core).
Axes of the slice: x: 4, y: 4, z: 8, core: 2. Of those that a mesh axis runs over, the one named last changes fastest.
Arguments:
- context_block_rows: bfloat16 [16384, 8192], P('ctx', 'tp'), may hold values from -16 to 16
- query_hidden_rows: bfloat16 [64, 8192], P(None, 'tp'), may hold values from -16 to 16
- query_token_positions: int32 [64], replicated, may hold values from 16384 to 16573, as said below
- query_bound: int32 [64], replicated, may hold values from 1 to 16384, as said below
- query_matrix: bfloat16 [8192, 8192], P('ctx', 'tp'), may hold values from -0.0625 to 0.0625
- key_matrix: bfloat16 [8192, 1024], P('ctx', 'tp'), may hold values from -0.0625 to 0.0625
- value_matrix: bfloat16 [8192, 1024], P('ctx', 'tp'), may hold values from -0.0625 to 0.0625
Outputs:
- block_out: bfloat16 [16384, 8192], P('ctx', 'tp')
- query_out: bfloat16 [64, 8192], P(None, 'tp')
The draws below stay inside these ranges and needn't reach their ends.
Inputs may be any that keep to these rules, and one draw needn't show every extreme that they name: query_token_positions rise strictly with the index; the first is 16384 and the last 16573. `query_bound`: some query token sees all 16384 context tokens.
All inputs are finite; a program needn't handle non-finite values.
Results may differ from the reference program's by a relative error of at most 0.0059.
The reference program's roundings to bfloat16 on the way count: a program that leaves them out, or rounds other values in their place, can miss the bound.
Values may be sent and summed in bfloat16 or wider, within the bound.
A program may use at most 128 MiB of HBM per device.

```python
import math
import jax
import jax.numpy as jnp
from jax import lax

MODEL_WIDTH = 8192
QUERY_HEADS = 64
KEY_HEADS = 8
HEAD_SIZE = 128
BLOCK_TOKENS = 512
QUERY_TOKENS = 64
CONTEXT_TOKENS = 16384
N_CTX = 32


def draw_rows(key, count):
    base = jnp.clip(jax.random.normal(jax.random.fold_in(key, 1), (count, MODEL_WIDTH), jnp.float32), -6.0, 6.0)
    return base


def draw_context_block_rows(key, part):
    return draw_rows(jax.random.fold_in(key, 11), CONTEXT_TOKENS).astype(jnp.bfloat16)


def draw_query_hidden_rows(key, part):
    return draw_rows(jax.random.fold_in(key, 12), QUERY_TOKENS).astype(jnp.bfloat16)


def draw_query_token_positions(key, part):
    offsets = jax.random.randint(jax.random.fold_in(key, 13), (QUERY_TOKENS,), 0, 3)
    index = jnp.arange(QUERY_TOKENS, dtype=jnp.int32)
    offsets = jnp.where((index == 0) | (index == QUERY_TOKENS - 1), 0, offsets)
    return (CONTEXT_TOKENS + 3 * index - offsets).astype(jnp.int32)


def draw_query_bound(key, part):
    bounds = jax.random.randint(jax.random.fold_in(key, 14), (QUERY_TOKENS,), 1, CONTEXT_TOKENS + 1)
    where_full = jax.random.randint(jax.random.fold_in(key, 15), (), 0, QUERY_TOKENS)
    return jnp.where(jnp.arange(QUERY_TOKENS) == where_full, CONTEXT_TOKENS, bounds).astype(jnp.int32)


def steps_of(own_key, extent, shards, low, top_value):
    def one(axis_at, shards_of):
        heights = jax.random.uniform(jax.random.fold_in(jax.random.fold_in(own_key, 6), axis_at), (shards_of,), jnp.float32, low / len(shards), top_value / len(shards))
        return jnp.repeat(jnp.exp(heights), extent[axis_at] // shards_of).reshape((-1,) + (1,) * (len(extent) - axis_at - 1))

    factor_of = one(*shards[0])
    for cut in shards[1:]:
        factor_of = factor_of * one(*cut)
    return factor_of


def normal_values(stream_key, shape, scale, most, cuts=(), kind=jnp.bfloat16):
    drawn = jax.random.normal(stream_key, shape, jnp.float32) * scale
    if len(cuts) > 0:
        drawn = steps_of(stream_key, shape, cuts, -0.22, 0.18) * drawn
    return jnp.clip(drawn, min=-most, max=most).astype(kind)


def setup_inputs(seed: int = 0) -> dict:
    key_list = jax.random.split(jax.random.key(seed), 8)
    context_block_rows = draw_context_block_rows(jax.random.fold_in(key_list[7], 71), 0)
    query_hidden_rows = draw_query_hidden_rows(jax.random.fold_in(key_list[7], 71), 0)
    query_token_positions = draw_query_token_positions(jax.random.fold_in(key_list[7], 71), 0)
    query_bound = draw_query_bound(jax.random.fold_in(key_list[7], 71), 0)
    query_matrix = normal_values(key_list[4], (MODEL_WIDTH, QUERY_HEADS * HEAD_SIZE), MODEL_WIDTH ** -0.5, 0.0625, ((0, 32), (1, 8)))
    key_matrix = normal_values(key_list[5], (MODEL_WIDTH, KEY_HEADS * HEAD_SIZE), MODEL_WIDTH ** -0.5, 0.0625, ((0, 32), (1, 8)))
    value_matrix = normal_values(key_list[6], (MODEL_WIDTH, KEY_HEADS * HEAD_SIZE), MODEL_WIDTH ** -0.5, 0.0625, ((0, 32), (1, 8)))
    return {"context_block_rows": context_block_rows, "query_hidden_rows": query_hidden_rows, "query_token_positions": query_token_positions, "query_bound": query_bound, "query_matrix": query_matrix, "key_matrix": key_matrix, "value_matrix": value_matrix}


def rope_table(half):
    values = []
    for index in range(half):
        freq = 500000.0 ** (-2.0 * index / (2.0 * half))
        wavelen = 2.0 * math.pi / freq
        if wavelen > 8192.0:
            values.append(freq / 8.0)
        elif wavelen < 2048.0:
            values.append(freq)
        else:
            smooth = (8192.0 / wavelen - 1.0) / 3.0
            values.append((1.0 - smooth) * freq / 8.0 + smooth * freq)
    return values

def apply_rotary(values, token_positions):
    half = values.shape[-1] // 2
    freqs = jnp.asarray(rope_table(half), jnp.float32)
    angle = token_positions.astype(jnp.float32)[:, None] * freqs[None, :]
    cosine = jnp.cos(angle)[:, None, :]
    sine = jnp.sin(angle)[:, None, :]
    first = values[..., :half]
    second = values[..., half:]
    return jnp.concatenate([first * cosine - second * sine, second * cosine + first * sine], -1)

def attend(query_heads_split, keys, values, valid):
    scale = 1.0 / math.sqrt(query_heads_split.shape[-1])
    scores = jnp.einsum('qkgd,skd->qkgs', query_heads_split.astype(jnp.float32), keys.astype(jnp.float32)) * scale
    scores = jnp.where(valid[:, None, None, :], scores, -1e+30)
    peak = lax.optimization_barrier(jnp.max(scores, -1))
    weights = jnp.exp(scores - peak[..., None])
    total = lax.optimization_barrier(jnp.sum(weights, -1))
    mixed = jnp.einsum('qkgs,skd->qkgd', weights.astype(jnp.bfloat16).astype(jnp.float32), values.astype(jnp.float32))
    return (peak, total, mixed)

def reference(context_block_rows, query_hidden_rows, query_token_positions, query_bound, query_matrix, key_matrix, value_matrix):
    head_group = QUERY_HEADS // KEY_HEADS
    token_positions = jnp.arange(CONTEXT_TOKENS, dtype=jnp.int32)
    query_heads_all = apply_rotary(jnp.dot(context_block_rows, query_matrix, preferred_element_type=jnp.float32).reshape(CONTEXT_TOKENS, QUERY_HEADS, HEAD_SIZE), token_positions).astype(jnp.bfloat16)
    key_heads_all = apply_rotary(jnp.dot(context_block_rows, key_matrix, preferred_element_type=jnp.float32).reshape(CONTEXT_TOKENS, KEY_HEADS, HEAD_SIZE), token_positions).astype(jnp.bfloat16)
    value_heads_all = jnp.dot(context_block_rows, value_matrix, preferred_element_type=jnp.float32).reshape(CONTEXT_TOKENS, KEY_HEADS, HEAD_SIZE).astype(jnp.bfloat16)
    anchor_key = key_heads_all[:BLOCK_TOKENS]
    anchor_value = value_heads_all[:BLOCK_TOKENS]
    lower = jnp.arange(BLOCK_TOKENS, dtype=jnp.int32)[:, None] >= jnp.arange(BLOCK_TOKENS, dtype=jnp.int32)[None, :]

    def one_block(block):
        block_start = (block * BLOCK_TOKENS).astype(jnp.int32)
        query_heads_split = lax.dynamic_slice_in_dim(query_heads_all, block_start, BLOCK_TOKENS, 0).reshape(BLOCK_TOKENS, KEY_HEADS, head_group, HEAD_SIZE)
        keys = jnp.concatenate([anchor_key, lax.dynamic_slice_in_dim(key_heads_all, block_start, BLOCK_TOKENS, 0)], 0)
        values = jnp.concatenate([anchor_value, lax.dynamic_slice_in_dim(value_heads_all, block_start, BLOCK_TOKENS, 0)], 0)
        valid = jnp.concatenate([jnp.broadcast_to(block > 0, (BLOCK_TOKENS, BLOCK_TOKENS)), lower], 1)
        peak, total, mixed = attend(query_heads_split, keys, values, valid)
        return (mixed / total[..., None]).astype(jnp.bfloat16).reshape(BLOCK_TOKENS, QUERY_HEADS * HEAD_SIZE)
    block_out = lax.map(one_block, jnp.arange(N_CTX, dtype=jnp.int32)).reshape(CONTEXT_TOKENS, QUERY_HEADS * HEAD_SIZE)
    query_token_rows = apply_rotary(jnp.dot(query_hidden_rows, query_matrix, preferred_element_type=jnp.float32).reshape(QUERY_TOKENS, QUERY_HEADS, HEAD_SIZE), query_token_positions).astype(jnp.bfloat16).reshape(QUERY_TOKENS, KEY_HEADS, head_group, HEAD_SIZE)
    key_token_rows = apply_rotary(jnp.dot(query_hidden_rows, key_matrix, preferred_element_type=jnp.float32).reshape(QUERY_TOKENS, KEY_HEADS, HEAD_SIZE), query_token_positions).astype(jnp.bfloat16)
    value_token_rows = jnp.dot(query_hidden_rows, value_matrix, preferred_element_type=jnp.float32).reshape(QUERY_TOKENS, KEY_HEADS, HEAD_SIZE).astype(jnp.bfloat16)

    def query_block(block):
        block_start = (block * BLOCK_TOKENS).astype(jnp.int32)
        keys = lax.dynamic_slice_in_dim(key_heads_all, block_start, BLOCK_TOKENS, 0)
        values = lax.dynamic_slice_in_dim(value_heads_all, block_start, BLOCK_TOKENS, 0)
        key_pos = block_start + jnp.arange(BLOCK_TOKENS, dtype=jnp.int32)
        valid = key_pos[None, :] < query_bound[:, None]
        return attend(query_token_rows, keys, values, valid)
    peaks, totals, mixeds = lax.map(query_block, jnp.arange(N_CTX, dtype=jnp.int32))
    top = lax.optimization_barrier(jnp.max(peaks, 0))
    scaled = jnp.exp(peaks - top[None])
    total_all = lax.optimization_barrier(jnp.sum(totals * scaled, 0))
    mixed_all = lax.optimization_barrier(jnp.sum(mixeds * scaled[..., None], 0))
    own = jnp.arange(QUERY_TOKENS, dtype=jnp.int32)
    self_peak, self_total, self_mixed = attend(query_token_rows, key_token_rows, value_token_rows, own[:, None] >= own[None, :])
    final = jnp.maximum(top, self_peak)
    w_ctx = jnp.exp(top - final)
    w_self = jnp.exp(self_peak - final)
    query_out = (mixed_all * w_ctx[..., None] + self_mixed * w_self[..., None]) / (total_all * w_ctx + self_total * w_self)[..., None]
    query_out = query_out.astype(jnp.bfloat16).reshape(QUERY_TOKENS, QUERY_HEADS * HEAD_SIZE)
    return (block_out, query_out)
```

```python
import math

import jax
import jax.numpy as jnp
import numpy as np
from jax import lax
from jax.experimental import pallas as pl
from jax.experimental.pallas import tpu as pltpu
from jax.sharding import PartitionSpec as P

MESH = pl.DeviceIdType.MESH
HEAD = 128
NX, NY, NZ = 4, 4, 8
N_CTX = NY * NZ
BLK = 512
QT = 64
ROWS = BLK + QT
SHARD = 256
CUT = 96
REST = SHARD - CUT
BLOCKS = 5
COLS = 256
CHUNK = ROWS // 4
FEATS = 1024
NEG = -1e30
POWER = math.log2(math.e) / math.sqrt(HEAD)
OWN = BLK // N_CTX
F32, BF16 = jnp.float32, jnp.bfloat16


def rope_table(half):
    values = []
    for index in range(half):
        freq = 500000.0 ** (-2.0 * index / (2.0 * half))
        wavelen = 2.0 * math.pi / freq
        if wavelen > 8192.0:
            values.append(freq / 8.0)
        elif wavelen < 2048.0:
            values.append(freq)
        else:
            smooth = (8192.0 / wavelen - 1.0) / 3.0
            values.append((1.0 - smooth) * freq / 8.0 + smooth * freq)
    return values


def bz_at(way, dist):
    return way * 4 + dist - 1


def by_at(off, way, stage):
    return 8 + (off % NZ) * 4 + way * 2 + stage - 1


def ay_at(way, stage):
    return 40 + way * 2 + stage - 1


def az_at(off, way, dist):
    return 44 + (off % NY) * 8 + way * 4 + dist - 1


PLACES = 76
SIGN = (1, -1)


def column(row):
    n = row.shape[1]
    same = lax.broadcasted_iota(jnp.int32, (n, n), 0) == lax.broadcasted_iota(jnp.int32, (n, n), 1)
    return jnp.sum(jnp.where(same, jnp.broadcast_to(row, (n, n)), 0.0), axis=1, keepdims=True)


def dot_nt(a, b):
    return lax.dot_general(a, b, (((1,), (1,)), ((), ())), preferred_element_type=F32)


def kernel(
    x_ref, xq_ref, wq_ref, wk_ref, wv_ref, pos_ref, bound_ref, freq_ref,
    out_ref, qout_ref,
    w_all, x_all, cos_s, sin_s, acc, kv, akv, q_s, qq_s, part, parts,
    local_sem, w_send, w_recv, x_send, x_recv, sib_send, sib_recv, a_send, a_recv,
    p_send, p_recv, r_send, r_recv,
):
    c = lax.axis_index("ctx")
    t = lax.axis_index("tp")
    y, z = lax.div(c, NZ), lax.rem(c, NZ)
    x, core = lax.div(t, 2), lax.rem(t, 2)

    def ctx_at(dy, dz):
        return lax.rem(y + dy + NY, NY) * NZ + lax.rem(z + dz + NZ, NZ)

    def tp_at(dx):
        return lax.rem(x + dx + NX, NX) * 2 + core

    sibling = x * 2 + 1 - core

    locals_ = [
        pltpu.make_async_copy(x_ref, x_all.at[t, pl.ds(0, BLK)], local_sem.at[0]),
        pltpu.make_async_copy(xq_ref, x_all.at[t, pl.ds(BLK, QT)], local_sem.at[1]),
    ]
    own = pl.ds(pl.multiple_of(c * SHARD, SHARD), SHARD)
    locals_.append(pltpu.make_async_copy(wk_ref, w_all.at[0, own, pl.ds(0, HEAD)], local_sem.at[2]))
    locals_.append(pltpu.make_async_copy(wv_ref, w_all.at[0, own, pl.ds(HEAD, HEAD)], local_sem.at[3]))
    for b in range(1, BLOCKS):
        locals_.append(
            pltpu.make_async_copy(
                wq_ref.at[:, pl.ds((b - 1) * COLS, COLS)], w_all.at[b, own], local_sem.at[3 + b]
            )
        )
    for copy in locals_:
        copy.start()

    barrier = pltpu.get_barrier_semaphore()

    @pl.loop(1, N_CTX)
    def _(d):
        pl.semaphore_signal(barrier, inc=1, device_id=(lax.rem(c + d, N_CTX), t), device_id_type=MESH)

    for other in (tp_at(1), tp_at(-1), sibling):
        pl.semaphore_signal(barrier, inc=1, device_id=(c, other), device_id_type=MESH)
    pl.semaphore_wait(barrier, N_CTX - 1 + 3)
    for copy in locals_:
        copy.wait()

    def rows_of(origin, first, count, dist, full, way):
        if dist == full:
            half = count // 2
            first, count = first + (half if way else 0), half
        return pl.ds(pl.multiple_of(origin * SHARD + first, 16), count)

    def w_copy(b, rows, target, line, place):
        piece = w_all.at[b, rows]
        return pltpu.make_async_remote_copy(
            src_ref=piece, dst_ref=piece, send_sem=w_send.at[b, line], recv_sem=w_recv.at[b, place],
            device_id=(target, t), device_id_type=MESH,
        )

    def bz(b, way, dist, hop):
        s = SIGN[way]
        rows = rows_of(ctx_at(0, -s * (dist - 1 + hop)), CUT, REST, dist, 4, way)
        return w_copy(b, rows, ctx_at(0, s), 2 + way, bz_at(way, dist))

    def by(b, off, way, stage, hop):
        s = SIGN[way]
        rows = rows_of(ctx_at(-s * (stage - 1 + hop), off), CUT, REST, stage, 2, way)
        return w_copy(b, rows, ctx_at(s, 0), way, by_at(off, way, stage))

    def ay(b, way, stage, hop):
        s = SIGN[way]
        rows = rows_of(ctx_at(-s * (stage - 1 + hop), 0), 0, CUT, stage, 2, way)
        return w_copy(b, rows, ctx_at(s, 0), way, ay_at(way, stage))

    def az(b, off, way, dist, hop):
        s = SIGN[way]
        rows = rows_of(ctx_at(off, -s * (dist - 1 + hop)), 0, CUT, dist, 4, way)
        return w_copy(b, rows, ctx_at(0, s), 2 + way, az_at(off, way, dist))

    def go(make, *args):
        make(*args, 0).start()

    def got(make, *args):
        make(*args, 1).wait_recv()

    def step(b, s):
        if s == 0:
            for way in (0, 1):
                go(bz, b, way, 1)
                go(ay, b, way, 1)
            for way in (0, 1):
                go(az, b, 0, way, 1)
                go(by, b, 0, way, 1)
            return
        if s <= 4:
            for way in (0, 1):
                got(bz, b, way, s)
                if s < 4:
                    go(bz, b, way, s + 1)
                    go(by, b, -SIGN[way] * s, 0, 1)
                    go(by, b, -SIGN[way] * s, 1, 1)
            if s == 4:
                go(by, b, 4, 0, 1)
                go(by, b, 4, 1, 1)
        if s == 1:
            for way in (0, 1):
                got(ay, b, way, 1)
                go(ay, b, way, 2)
                go(az, b, -SIGN[way], 0, 1)
                go(az, b, -SIGN[way], 1, 1)
        if s == 2:
            got(ay, b, 0, 2)
            got(ay, b, 1, 2)
            go(az, b, 2, 0, 1)
            go(az, b, 2, 1, 1)
        for off, since in ((0, 0), (1, 1), (-1, 1), (2, 2)):
            dist = s - since
            if 1 <= dist <= 4:
                for way in (0, 1):
                    got(az, b, off, way, dist)
                    if dist < 4:
                        go(az, b, off, way, dist + 1)
        for group in range(5):
            offs = (0,) if group == 0 else (4,) if group == 4 else (-group, group)
            stage = s - group
            if 1 <= stage <= 2:
                for off in offs:
                    for way in (0, 1):
                        got(by, b, off, way, stage)
                        if stage == 1:
                            go(by, b, off, way, 2)

    def x_copy(dx, rows, target, send, recv):
        piece = x_all.at[tp_at(dx), rows]
        return pltpu.make_async_remote_copy(
            src_ref=piece, dst_ref=piece, send_sem=send, recv_sem=recv,
            device_id=(c, target), device_id_type=MESH,
        )

    def x_near(way, chunk, hop):
        return x_copy(-SIGN[way] * hop, pl.ds(chunk * CHUNK, CHUNK), tp_at(SIGN[way]), x_send.at[way, chunk], x_recv.at[way, chunk])

    def x_far(way, chunk, hop):
        return x_copy(-SIGN[way] * (1 + hop), pl.ds(chunk * CHUNK, CHUNK), tp_at(SIGN[way]), x_send.at[2, chunk], x_recv.at[2, chunk])

    FAR = ((0, 1), (2, 3))

    def x_across(dx):
        piece = x_all.at[tp_at(dx)]
        return pltpu.make_async_remote_copy(
            src_ref=piece, dst_ref=piece, send_sem=sib_send.at[dx % 4], recv_sem=sib_recv.at[dx % 4],
            device_id=(c, sibling), device_id_type=MESH,
        )

    def x_arrives(dx):
        piece = x_all.at[lax.rem(x + dx + NX, NX) * 2 + 1 - core]
        return pltpu.make_async_remote_copy(
            src_ref=piece, dst_ref=piece, send_sem=sib_send.at[dx % 4], recv_sem=sib_recv.at[dx % 4],
            device_id=(c, sibling), device_id_type=MESH,
        )

    def x_first():
        for way in (0, 1):
            for chunk in FAR[way] + FAR[1 - way]:
                x_near(way, chunk, 0).start()
        x_across(0).start()

    def x_second():
        for way in (0, 1):
            for chunk in FAR[way]:
                x_near(way, chunk, 1).wait_recv()
                x_far(way, chunk, 0).start()

    def x_third():
        for way in (0, 1):
            for chunk in FAR[1 - way]:
                x_near(way, chunk, 1).wait_recv()
            x_across(-SIGN[way]).start()

    def x_fourth():
        for way in (0, 1):
            for chunk in FAR[way]:
                x_far(way, chunk, 1).wait_recv()
        x_across(2).start()

    def x_last():
        for dx in (0, 1, -1, 2):
            x_arrives(dx).wait_recv()

    def angles(first, positions):
        angle = positions * freq_ref[...]
        lane = lax.broadcasted_iota(jnp.int32, angle.shape, 1)
        cosine, sine = jnp.cos(angle), jnp.sin(angle)
        rows = pl.ds(first, angle.shape[0])
        cos_s[rows, :] = cosine
        sin_s[rows, :] = jnp.where(lane < HEAD // 2, -sine, sine)

    def block_angles(first, count):
        place = lax.broadcasted_iota(jnp.int32, (count, HEAD), 0) + (c * BLK + first)
        angles(first, place.astype(F32))

    def query_angles():
        place = column(pos_ref[...].astype(F32))
        angles(BLK, jnp.broadcast_to(place, (QT, HEAD)))

    def rotate(u):
        return u * cos_s[...] + pltpu.roll(u, HEAD // 2, 1) * sin_s[...]

    def project(b):
        acc[...] = jnp.zeros_like(acc)

        @pl.loop(0, 8)
        def _(s):
            acc[...] += jnp.dot(
                x_all[s],
                w_all[b, pl.ds(pl.multiple_of(s * FEATS, FEATS), FEATS), :],
                preferred_element_type=F32,
            )

    def project_kv():
        project(0)
        kv[:, :HEAD] = rotate(acc[:, :HEAD]).astype(BF16)
        kv[:, HEAD:] = acc[:, HEAD:].astype(BF16)

    def project_q(pair):
        project(pair + 1)
        for hh in range(2):
            turned = rotate(acc[:, hh * HEAD : (hh + 1) * HEAD]).astype(BF16)
            q_s[:, hh * HEAD : (hh + 1) * HEAD] = turned[:BLK]
            qq_s[pl.ds(pl.multiple_of((pair * 2 + hh) * QT, QT), QT), :] = turned[BLK:]

    def send_part(owner):
        return pltpu.make_async_remote_copy(
            src_ref=part.at[pl.ds(pl.multiple_of(owner * OWN, OWN), OWN)],
            dst_ref=parts.at[c], send_sem=p_send.at[owner], recv_sem=p_recv.at[c],
            device_id=(owner, t), device_id_type=MESH,
        )

    def query_part(pair):
        rows = pl.ds(pl.multiple_of(pair * 2 * QT, 2 * QT), 2 * QT)
        scores = dot_nt(qq_s[rows, :], kv[:BLK, :HEAD])
        bound = column(bound_ref[...].astype(F32))
        bound = jnp.concatenate([bound, bound], 0)
        place = (lax.broadcasted_iota(jnp.int32, scores.shape, 1) + c * BLK).astype(F32)
        scores = jnp.where(place < bound, scores, NEG)
        peak = jnp.max(scores, 1, keepdims=True)
        weights = jnp.exp2((scores - peak) * POWER)
        total = jnp.sum(weights, 1, keepdims=True)
        mixed = jnp.dot(weights.astype(BF16), kv[:BLK, HEAD:], preferred_element_type=F32)
        lane = lax.broadcasted_iota(jnp.int32, mixed.shape, 1)
        part[rows, :HEAD] = mixed
        part[rows, HEAD:] = jnp.where(lane < HEAD // 2, peak, total)

        @pl.loop(0, 8)
        def _(n):
            owner = pair * 8 + n

            @pl.when(owner != c)
            def _():
                send_part(owner).start()

            @pl.when(owner == c)
            def _():
                parts[c] = part[pl.ds(pl.multiple_of(c * OWN, OWN), OWN), :]

    def attend(pair, hh):
        head = pair * 2 + hh
        bias = jnp.where(c > 0, 0.0, NEG).astype(F32)
        tile = BLK // 2
        for n in range(2):
            span = (n + 1) * tile
            q = q_s[n * tile : span, hh * HEAD : (hh + 1) * HEAD]
            far = dot_nt(q, akv[:, :HEAD])
            near = dot_nt(q, kv[:span, :HEAD])
            row = lax.broadcasted_iota(jnp.int32, near.shape, 0) + n * tile
            near = jnp.where(row >= lax.broadcasted_iota(jnp.int32, near.shape, 1), near, NEG)
            peak = jnp.maximum(
                jnp.max(far, 1, keepdims=True) + bias, jnp.max(near, 1, keepdims=True)
            )
            far = jnp.exp2((far - (peak - bias)) * POWER)
            near = jnp.exp2((near - peak) * POWER)
            total = jnp.sum(far, 1, keepdims=True) + jnp.sum(near, 1, keepdims=True)
            mixed = jnp.dot(far.astype(BF16), akv[:, HEAD:], preferred_element_type=F32)
            mixed += jnp.dot(near.astype(BF16), kv[:span, HEAD:], preferred_element_type=F32)
            out_ref[n * tile : span, pl.ds(pl.multiple_of(head * HEAD, HEAD), HEAD)] = (
                mixed / total
            ).astype(BF16)

    depth = jnp.where(y == 3, 1, y) + jnp.minimum(z, NZ - z)

    def anchor_copy(first, count, target, line, place):
        piece = akv.at[pl.ds(first, count)]
        return pltpu.make_async_remote_copy(
            src_ref=piece, dst_ref=piece, send_sem=a_send.at[line], recv_sem=a_recv.at[place],
            device_id=(target, t), device_id_type=MESH,
        )

    HALF = BLK // 2

    def anchor_sends(act):
        @pl.when((z == 0) & (y < 2))
        def _():
            act(anchor_copy(0, BLK, ctx_at(1, 0), 0, 0))

        @pl.when(c == 0)
        def _():
            act(anchor_copy(0, BLK, ctx_at(-1, 0), 1, 0))

        @pl.when(z < 3)
        def _():
            act(anchor_copy(0, BLK, ctx_at(0, 1), 2, 0))

        @pl.when(z == 3)
        def _():
            act(anchor_copy(0, HALF, ctx_at(0, 1), 2, 0))

        @pl.when((z > 5) | (z == 0))
        def _():
            act(anchor_copy(0, BLK, ctx_at(0, -1), 3, 0))

        @pl.when(z == 5)
        def _():
            act(anchor_copy(HALF, HALF, ctx_at(0, -1), 3, 1))

    def anchor_pass():
        @pl.when(z != 4)
        def _():
            anchor_copy(0, BLK, ctx_at(0, 1), 2, 0).wait_recv()

        @pl.when(z == 4)
        def _():
            anchor_copy(0, HALF, ctx_at(0, 1), 2, 0).wait_recv()
            anchor_copy(HALF, HALF, ctx_at(0, 1), 2, 1).wait_recv()

        anchor_sends(lambda copy: copy.start())

    x_first()

    @pl.loop(0, BLOCKS + 1)
    def _(j):
        for r in range(4):
            if r < 3:

                @pl.when(j >= 1)
                def _():
                    step(j - 1, r + 4)

            @pl.when(j < BLOCKS)
            def _():
                step(j, r)

            @pl.when((depth > 0) & (depth == 4 * j + r - 8))
            def _():
                anchor_pass()

            @pl.when(j == 0)
            def _():
                block_angles(r * (BLK // 4), BLK // 4)
                if r == 3:
                    query_angles()
                    x_second()

            @pl.when(j == 1)
            def _():
                if r == 1:
                    x_third()
                if r == 3:
                    x_fourth()

            if r == 0:

                @pl.when(j == 2)
                def _():
                    x_last()
                    project_kv()

                    @pl.when(c == 0)
                    def _():
                        akv[...] = kv[:BLK, :]
                        anchor_sends(lambda copy: copy.start())

            if r == 2:

                @pl.when(j == 3)
                def _():
                    attend(0, 0)
                    attend(0, 1)

            if r == 0:

                @pl.when(j >= 4)
                def _():
                    attend(j - 3, 0)
                    attend(j - 3, 1)

            if r == 3:

                @pl.when(j >= 2)
                def _():
                    project_q(j - 2)
                    query_part(j - 2)

    attend(3, 0)
    attend(3, 1)

    @pl.loop(0, N_CTX)
    def _(n):
        @pl.when(n != c)
        def _():
            piece = parts.at[n]
            pltpu.make_async_remote_copy(
                src_ref=piece, dst_ref=piece, send_sem=p_send.at[n], recv_sem=p_recv.at[n],
                device_id=(n, t), device_id_type=MESH,
            ).wait_recv()

    peaks = parts[:, :, HEAD : HEAD + 1]
    top = jnp.max(peaks, 0)
    scaled = jnp.exp2((peaks - top[None]) * POWER)
    total_all = jnp.sum(parts[:, :, HEAD + HEAD // 2 : HEAD + HEAD // 2 + 1] * scaled, 0)
    mixed_all = jnp.sum(parts[:, :, :HEAD] * scaled, 0)

    first = lax.rem(c, QT // OWN) * OWN
    mine = qq_s[pl.ds(pl.multiple_of(c * OWN, OWN), OWN), :]
    scores = dot_nt(mine, kv[BLK:, :HEAD])
    row = lax.broadcasted_iota(jnp.int32, scores.shape, 0) + first
    scores = jnp.where(row >= lax.broadcasted_iota(jnp.int32, scores.shape, 1), scores, NEG)
    peak = jnp.max(scores, 1, keepdims=True)
    weights = jnp.exp2((scores - peak) * POWER)
    total = jnp.sum(weights, 1, keepdims=True)
    mixed = jnp.dot(weights.astype(BF16), kv[BLK:, HEAD:], preferred_element_type=F32)
    final = jnp.maximum(top, peak)
    w_ctx = jnp.exp2((top - final) * POWER)
    w_self = jnp.exp2((peak - final) * POWER)
    done = (mixed_all * w_ctx + mixed * w_self) / (total_all * w_ctx + total * w_self)

    def result_at(n):
        return qout_ref.at[
            pl.ds(pl.multiple_of(lax.rem(n, QT // OWN) * OWN, OWN), OWN),
            pl.ds(pl.multiple_of(lax.div(n, QT // OWN) * HEAD, HEAD), HEAD),
        ]

    def result_copy(source, target):
        piece = result_at(source)
        return pltpu.make_async_remote_copy(
            src_ref=piece, dst_ref=piece, send_sem=r_send.at[target], recv_sem=r_recv.at[source],
            device_id=(target, t), device_id_type=MESH,
        )

    result_at(c)[...] = done.astype(BF16)

    @pl.loop(1, N_CTX)
    def _(d):
        result_copy(c, lax.rem(c + d, N_CTX)).start()

    @pl.loop(1, N_CTX)
    def _(d):
        other = lax.rem(c + d, N_CTX)
        result_copy(other, other).wait_recv()

    @pl.loop(1, N_CTX)
    def _(d):
        other = lax.rem(c + d, N_CTX)
        result_copy(c, other).wait_send()
        send_part(other).wait_send()

    @pl.loop(0, BLOCKS)
    def _(b):
        for line in range(4):
            rows = (3 * CUT // 2 + 8 * (3 * REST // 2)) if line < 2 else 7 * REST // 2 + 4 * (7 * CUT // 2)
            w_copy(b, pl.ds(0, rows), ctx_at(1, 0), line, 0).wait_send()

    for way in (0, 1):
        for chunk in range(4):
            x_near(way, chunk, 0).wait_send()
        for chunk in FAR[way]:
            x_far(way, chunk, 0).wait_send()
    for dx in (0, 1, -1, 2):
        x_across(dx).wait_send()
    anchor_sends(lambda copy: copy.wait_send())


def on_device(rows, query_rows, positions, bound, wq, wk, wv):
    freq = np.asarray(rope_table(HEAD // 2) * 2, np.float32)[None]
    anywhere = pl.BlockSpec(memory_space=pl.ANY)
    vmem = pl.BlockSpec(memory_space=pltpu.VMEM)
    dma = pltpu.SemaphoreType.DMA
    return pl.pallas_call(
        kernel,
        out_shape=(
            jax.ShapeDtypeStruct((BLK, 8 * HEAD), BF16),
            jax.ShapeDtypeStruct((QT, 8 * HEAD), BF16),
        ),
        in_specs=[anywhere] * 5 + [vmem] * 3,
        out_specs=(vmem, vmem),
        scratch_shapes=[
            pltpu.VMEM((BLOCKS, N_CTX * SHARD, COLS), BF16),
            pltpu.VMEM((8, ROWS, FEATS), BF16),
            pltpu.VMEM((ROWS, HEAD), F32),
            pltpu.VMEM((ROWS, HEAD), F32),
            pltpu.VMEM((ROWS, COLS), F32),
            pltpu.VMEM((ROWS, COLS), BF16),
            pltpu.VMEM((BLK, COLS), BF16),
            pltpu.VMEM((BLK, COLS), BF16),
            pltpu.VMEM((8 * QT, HEAD), BF16),
            pltpu.VMEM((8 * QT, 2 * HEAD), F32),
            pltpu.VMEM((N_CTX, OWN, 2 * HEAD), F32),
            dma((3 + BLOCKS,)),
            dma((BLOCKS, 4)),
            dma((BLOCKS, PLACES)),
            dma((3, 4)),
            dma((3, 4)),
            dma((4,)),
            dma((4,)),
            dma((4,)),
            dma((2,)),
            dma((N_CTX,)),
            dma((N_CTX,)),
            dma((N_CTX,)),
            dma((N_CTX,)),
        ],
        compiler_params=pltpu.CompilerParams(
            collective_id=0, has_side_effects=True, vmem_limit_bytes=56 << 20
        ),
        name="star_prefill",
    )(rows, query_rows, wq, wk, wv, positions[None], bound[None], freq)


def solution(mesh):
    placed = (
        P("ctx", "tp"),
        P(None, "tp"),
        P(),
        P(),
        P("ctx", "tp"),
        P("ctx", "tp"),
        P("ctx", "tp"),
    )
    return jax.shard_map(
        on_device,
        mesh=mesh,
        in_specs=placed,
        out_specs=(P("ctx", "tp"), P(None, "tp")),
        check_vma=False,
    )
```

```python
import math

import jax
import jax.numpy as jnp
import numpy as np
from jax import lax
from jax.experimental import pallas as pl
from jax.experimental.pallas import tpu as pltpu
from jax.sharding import PartitionSpec as P

MESH = pl.DeviceIdType.MESH
HEAD = 128
NX, NY, NZ = 4, 4, 8
N_CTX = NY * NZ
BLK = 512
QT = 64
ROWS = BLK + QT
SHARD = 256
CUT = 96
REST = SHARD - CUT
BLOCKS = 4
TAILS = 2
PAIRS = 3
COLS = 256
CHUNK = ROWS // 4
FEATS = 1024
NEG = -1e30
POWER = math.log2(math.e) / math.sqrt(HEAD)
OWN = BLK // N_CTX
F32, BF16 = jnp.float32, jnp.bfloat16


def rope_table(half):
    values = []
    for index in range(half):
        freq = 500000.0 ** (-2.0 * index / (2.0 * half))
        wavelen = 2.0 * math.pi / freq
        if wavelen > 8192.0:
            values.append(freq / 8.0)
        elif wavelen < 2048.0:
            values.append(freq)
        else:
            smooth = (8192.0 / wavelen - 1.0) / 3.0
            values.append((1.0 - smooth) * freq / 8.0 + smooth * freq)
    return values


def bz_at(dist):
    return dist - 1


def by_at(off, stage):
    return 4 + (off % NZ) * 2 + stage - 1


def ay_at(stage):
    return 20 + stage - 1


def az_at(off, dist):
    return 22 + (off % NY) * 4 + dist - 1


PLACES = 38
SIGN = (1, -1)


def column(row):
    n = row.shape[1]
    same = lax.broadcasted_iota(jnp.int32, (n, n), 0) == lax.broadcasted_iota(jnp.int32, (n, n), 1)
    return jnp.sum(jnp.where(same, jnp.broadcast_to(row, (n, n)), 0.0), axis=1, keepdims=True)


def dot_nt(a, b):
    return lax.dot_general(a, b, (((1,), (1,)), ((), ())), preferred_element_type=F32)


def kernel(
    x_ref, xq_ref, wq_ref, wk_ref, wv_ref, pos_ref, bound_ref, freq_ref,
    out_ref, qout_ref,
    w_all, w_tail, x_all, cos_s, sin_s, acc, kv, akv, q_s, qq_s, part, parts,
    local_sem, w_send, w_recv, x_send, x_recv, sib_send, sib_recv, a_send, a_recv,
    p_send, p_recv, r_send, r_recv,
):
    c = lax.axis_index("ctx")
    t = lax.axis_index("tp")
    y, z = lax.div(c, NZ), lax.rem(c, NZ)
    x, core = lax.div(t, 2), lax.rem(t, 2)

    def ctx_at(dy, dz):
        return lax.rem(y + dy + NY, NY) * NZ + lax.rem(z + dz + NZ, NZ)

    def tp_at(dx):
        return lax.rem(x + dx + NX, NX) * 2 + core

    sibling = x * 2 + 1 - core

    locals_ = [
        pltpu.make_async_copy(x_ref, x_all.at[t, pl.ds(0, BLK)], local_sem.at[0]),
        pltpu.make_async_copy(xq_ref, x_all.at[t, pl.ds(BLK, QT)], local_sem.at[1]),
    ]
    own = pl.ds(pl.multiple_of(c * SHARD, SHARD), SHARD)
    locals_.append(pltpu.make_async_copy(wk_ref, w_all.at[0, own, pl.ds(0, HEAD)], local_sem.at[2]))
    locals_.append(pltpu.make_async_copy(wv_ref, w_all.at[0, own, pl.ds(HEAD, HEAD)], local_sem.at[3]))
    for b in range(1, BLOCKS):
        locals_.append(
            pltpu.make_async_copy(
                wq_ref.at[:, pl.ds((b - 1) * COLS, COLS)], w_all.at[b, own], local_sem.at[3 + b]
            )
        )
    for b in range(TAILS):
        locals_.append(
            pltpu.make_async_copy(
                wq_ref.at[:, pl.ds(PAIRS * COLS + b * HEAD, HEAD)], w_tail.at[b, own], local_sem.at[3 + BLOCKS + b]
            )
        )
    for copy in locals_:
        copy.start()

    barrier = pltpu.get_barrier_semaphore()

    @pl.loop(1, N_CTX)
    def _(d):
        pl.semaphore_signal(barrier, inc=1, device_id=(lax.rem(c + d, N_CTX), t), device_id_type=MESH)

    for other in (tp_at(1), tp_at(-1), sibling):
        pl.semaphore_signal(barrier, inc=1, device_id=(c, other), device_id_type=MESH)
    pl.semaphore_wait(barrier, N_CTX - 1 + 3)
    for copy in locals_:
        copy.wait()

    def rows_of(origin, first, count, dist, full, way):
        if dist == full:
            half = count // 2
            first, count = first + (half if way else 0), half
        return pl.ds(pl.multiple_of(origin * SHARD + first, 16), count)

    def w_copy(blk, rows, target, line, place):
        ref, sem = blk
        piece = ref.at[rows]
        return pltpu.make_async_remote_copy(
            src_ref=piece, dst_ref=piece, send_sem=w_send.at[sem, line], recv_sem=w_recv.at[sem, place],
            device_id=(target, t), device_id_type=MESH,
        )

    def wide(j):
        return w_all.at[j], j

    def tail(n):
        return w_tail.at[n], BLOCKS + n

    def bz(blk, way, dist):
        s = SIGN[way]
        rows = rows_of(ctx_at(0, -s * (dist - 1)), CUT, REST, dist, 4, way)
        w_copy(blk, rows, ctx_at(0, s), 2 + way, bz_at(dist)).start()

    def by(blk, off, way, stage):
        s = SIGN[way]
        rows = rows_of(ctx_at(-s * (stage - 1), off), CUT, REST, stage, 2, way)
        w_copy(blk, rows, ctx_at(s, 0), way, by_at(off, stage)).start()

    def ay(blk, way, stage):
        s = SIGN[way]
        rows = rows_of(ctx_at(-s * (stage - 1), 0), 0, CUT, stage, 2, way)
        w_copy(blk, rows, ctx_at(s, 0), way, ay_at(stage)).start()

    def az(blk, off, way, dist):
        s = SIGN[way]
        rows = rows_of(ctx_at(off, -s * (dist - 1)), 0, CUT, dist, 4, way)
        w_copy(blk, rows, ctx_at(0, s), 2 + way, az_at(off, dist)).start()

    def both(make, blk, *args):
        *front, last = args
        for way in (0, 1):
            make(blk, *front, way, last)

    def got(blk, place, count):
        w_copy(blk, pl.ds(0, count), ctx_at(1, 0), 0, place).wait_recv()

    def step(blk, s):
        if s == 0:
            both(bz, blk, 1)
            both(ay, blk, 1)
            both(az, blk, 0, 1)
            both(by, blk, 0, 1)
            return
        if s <= 4:
            got(blk, bz_at(s), 2 * REST if s < 4 else REST)
            if s < 4:
                both(bz, blk, s + 1)
                both(by, blk, -s, 1)
                both(by, blk, s, 1)
            else:
                both(by, blk, 4, 1)
        if s == 1:
            got(blk, ay_at(1), 2 * CUT)
            both(ay, blk, 2)
            both(az, blk, -1, 1)
            both(az, blk, 1, 1)
        if s == 2:
            got(blk, ay_at(2), CUT)
            both(az, blk, 2, 1)
        for off, since in ((0, 0), (1, 1), (-1, 1), (2, 2)):
            dist = s - since
            if 1 <= dist <= 4:
                got(blk, az_at(off, dist), 2 * CUT if dist < 4 else CUT)
                if dist < 4:
                    both(az, blk, off, dist + 1)
        for group in range(5):
            offs = (0,) if group == 0 else (4,) if group == 4 else (-group, group)
            stage = s - group
            if 1 <= stage <= 2:
                for off in offs:
                    got(blk, by_at(off, stage), 2 * REST if stage == 1 else REST)
                    if stage == 1:
                        both(by, blk, off, 2)

    def x_copy(dx, rows, target, send, recv):
        piece = x_all.at[tp_at(dx), rows]
        return pltpu.make_async_remote_copy(
            src_ref=piece, dst_ref=piece, send_sem=send, recv_sem=recv,
            device_id=(c, target), device_id_type=MESH,
        )

    def x_near(way, chunk, hop):
        return x_copy(-SIGN[way] * hop, pl.ds(chunk * CHUNK, CHUNK), tp_at(SIGN[way]), x_send.at[way, chunk], x_recv.at[way, chunk])

    def x_far(way, chunk, hop):
        return x_copy(-SIGN[way] * (1 + hop), pl.ds(chunk * CHUNK, CHUNK), tp_at(SIGN[way]), x_send.at[2, chunk], x_recv.at[2, chunk])

    FAR = ((0, 1), (2, 3))

    def x_across(dx):
        piece = x_all.at[tp_at(dx)]
        return pltpu.make_async_remote_copy(
            src_ref=piece, dst_ref=piece, send_sem=sib_send.at[dx % 4], recv_sem=sib_recv.at[dx % 4],
            device_id=(c, sibling), device_id_type=MESH,
        )

    def x_arrives(dx):
        piece = x_all.at[lax.rem(x + dx + NX, NX) * 2 + 1 - core]
        return pltpu.make_async_remote_copy(
            src_ref=piece, dst_ref=piece, send_sem=sib_send.at[dx % 4], recv_sem=sib_recv.at[dx % 4],
            device_id=(c, sibling), device_id_type=MESH,
        )

    def x_first():
        for way in (0, 1):
            for chunk in FAR[way] + FAR[1 - way]:
                x_near(way, chunk, 0).start()
        x_across(0).start()

    def x_second():
        for way in (0, 1):
            for chunk in FAR[way]:
                x_near(way, chunk, 1).wait_recv()
                x_far(way, chunk, 0).start()

    def x_third():
        for way in (0, 1):
            for chunk in FAR[1 - way]:
                x_near(way, chunk, 1).wait_recv()
            x_across(-SIGN[way]).start()

    def x_fourth():
        for way in (0, 1):
            for chunk in FAR[way]:
                x_far(way, chunk, 1).wait_recv()
        x_across(2).start()

    def x_last():
        for dx in (0, 1, -1, 2):
            x_arrives(dx).wait_recv()

    def angles(first, positions):
        angle = positions * freq_ref[...]
        lane = lax.broadcasted_iota(jnp.int32, angle.shape, 1)
        cosine, sine = jnp.cos(angle), jnp.sin(angle)
        rows = pl.ds(first, angle.shape[0])
        cos_s[rows, :] = cosine
        sin_s[rows, :] = jnp.where(lane < HEAD // 2, -sine, sine)

    def block_angles(first, count):
        place = lax.broadcasted_iota(jnp.int32, (count, HEAD), 0) + (c * BLK + first)
        angles(first, place.astype(F32))

    def query_angles():
        place = column(pos_ref[...].astype(F32))
        angles(BLK, jnp.broadcast_to(place, (QT, HEAD)))

    def project(weights, first, count, columns):
        acc[first : first + count, :columns] = jnp.zeros((count, columns), F32)

        @pl.loop(0, 8)
        def _(s):
            acc[first : first + count, :columns] += jnp.dot(
                x_all[s, first : first + count],
                weights[pl.ds(pl.multiple_of(s * FEATS, FEATS), FEATS), :],
                preferred_element_type=F32,
            )

    def rotate(first, count, lane):
        u = acc[first : first + count, lane : lane + HEAD]
        turned = u * cos_s[first : first + count] + pltpu.roll(u, HEAD // 2, 1) * sin_s[first : first + count]
        return turned.astype(BF16)

    def project_kv():
        project(w_all.at[0], 0, ROWS, COLS)
        kv[:, :HEAD] = rotate(0, ROWS, 0)
        kv[:, HEAD:] = acc[:, HEAD:].astype(BF16)

    def keep_block(head, lane):
        q_s[head] = rotate(0, BLK, lane)

    def keep_query(head, lane):
        qq_s[pl.ds(pl.multiple_of(head * QT, QT), QT), :] = rotate(BLK, QT, lane)

    def project_pair(pair):
        project(w_all.at[pair + 1], 0, ROWS, COLS)
        for hh in range(2):
            keep_block(pair * 2 + hh, hh * HEAD)
            keep_query(pair * 2 + hh, hh * HEAD)

    def send_part(owner):
        return pltpu.make_async_remote_copy(
            src_ref=part.at[pl.ds(pl.multiple_of(owner * OWN, OWN), OWN)],
            dst_ref=parts.at[c], send_sem=p_send.at[owner], recv_sem=p_recv.at[c],
            device_id=(owner, t), device_id_type=MESH,
        )

    def query_part(head, heads):
        rows = pl.ds(pl.multiple_of(head * QT, QT), heads * QT)
        scores = dot_nt(qq_s[rows, :], kv[:BLK, :HEAD])
        bound = column(bound_ref[...].astype(F32))
        bound = jnp.concatenate([bound] * heads, 0)
        place = (lax.broadcasted_iota(jnp.int32, scores.shape, 1) + c * BLK).astype(F32)
        scores = jnp.where(place < bound, scores, NEG)
        peak = jnp.max(scores, 1, keepdims=True)
        weights = jnp.exp2((scores - peak) * POWER)
        total = jnp.sum(weights, 1, keepdims=True)
        mixed = jnp.dot(weights.astype(BF16), kv[:BLK, HEAD:], preferred_element_type=F32)
        lane = lax.broadcasted_iota(jnp.int32, mixed.shape, 1)
        part[rows, :HEAD] = mixed
        part[rows, HEAD:] = jnp.where(lane < HEAD // 2, peak, total)

        @pl.loop(0, heads * QT // OWN)
        def _(n):
            owner = head * (QT // OWN) + n

            @pl.when(owner != c)
            def _():
                send_part(owner).start()

            @pl.when(owner == c)
            def _():
                parts[c] = part[pl.ds(pl.multiple_of(c * OWN, OWN), OWN), :]

    def attend(head):
        bias = jnp.where(c > 0, 0.0, NEG).astype(F32)
        tile = BLK // 2
        for n in range(2):
            span = (n + 1) * tile
            q = q_s[head, n * tile : span, :]
            far = dot_nt(q, akv[:, :HEAD])
            near = dot_nt(q, kv[:span, :HEAD])
            row = lax.broadcasted_iota(jnp.int32, near.shape, 0) + n * tile
            near = jnp.where(row >= lax.broadcasted_iota(jnp.int32, near.shape, 1), near, NEG)
            peak = jnp.maximum(
                jnp.max(far, 1, keepdims=True) + bias, jnp.max(near, 1, keepdims=True)
            )
            far = jnp.exp2((far - (peak - bias)) * POWER)
            near = jnp.exp2((near - peak) * POWER)
            total = jnp.sum(far, 1, keepdims=True) + jnp.sum(near, 1, keepdims=True)
            mixed = jnp.dot(far.astype(BF16), akv[:, HEAD:], preferred_element_type=F32)
            mixed += jnp.dot(near.astype(BF16), kv[:span, HEAD:], preferred_element_type=F32)
            out_ref[n * tile : span, pl.ds(pl.multiple_of(head * HEAD, HEAD), HEAD)] = (
                mixed / total
            ).astype(BF16)

    depth = jnp.where(y == 3, 1, y) + jnp.minimum(z, NZ - z)

    def anchor_copy(first, count, target, line, place):
        piece = akv.at[pl.ds(first, count)]
        return pltpu.make_async_remote_copy(
            src_ref=piece, dst_ref=piece, send_sem=a_send.at[line], recv_sem=a_recv.at[place],
            device_id=(target, t), device_id_type=MESH,
        )

    PIECE = BLK // 4
    HALF = BLK // 2

    def anchor_lines(act):
        @pl.when((z == 0) & (y < 2))
        def _():
            act(ctx_at(1, 0), 0)

        @pl.when(c == 0)
        def _():
            act(ctx_at(-1, 0), 1)

        @pl.when(z < 3)
        def _():
            act(ctx_at(0, 1), 2)

        @pl.when((z > 5) | (z == 0))
        def _():
            act(ctx_at(0, -1), 3)

    def anchor_piece(k, target, line):
        return anchor_copy(pl.multiple_of(k * PIECE, PIECE), PIECE, target, line, k)

    def anchor_step(g):
        k = g - depth

        @pl.when((k >= 0) & (k < 4))
        def _():
            @pl.when(depth > 0)
            def _():
                anchor_piece(k, ctx_at(0, 1), 2).wait_recv()

            anchor_lines(lambda target, line: anchor_piece(k, target, line).start())

            @pl.when((z == 3) & (k < 2))
            def _():
                anchor_piece(k, ctx_at(0, 1), 2).start()

            @pl.when((z == 5) & (k >= 2))
            def _():
                anchor_piece(k, ctx_at(0, -1), 3).start()

    def anchor_end():
        anchor_lines(lambda target, line: anchor_copy(0, BLK, target, line, 0).wait_send())

        @pl.when(z == 3)
        def _():
            anchor_copy(0, HALF, ctx_at(0, 1), 2, 0).wait_send()

        @pl.when(z == 5)
        def _():
            anchor_copy(0, HALF, ctx_at(0, -1), 3, 0).wait_send()

    x_first()

    @pl.loop(0, BLOCKS)
    def _(j):
        for r in range(4):
            if r < 3:

                @pl.when(j >= 1)
                def _():
                    step(wide(j - 1), r + 4)

            step(wide(j), r)

            if r == 0:

                @pl.when(j == 2)
                def _():
                    x_last()
                    project_kv()

                    @pl.when(c == 0)
                    def _():
                        akv[...] = kv[:BLK, :]

            anchor_step(4 * j + r - 8)

            @pl.when(j == 0)
            def _():
                block_angles(r * (BLK // 4), BLK // 4)
                if r == 3:
                    query_angles()
                    x_second()

            @pl.when(j == 1)
            def _():
                if r == 1:
                    x_third()
                if r == 3:
                    x_fourth()

            if r == 3:

                @pl.when(j >= 2)
                def _():
                    project_pair(j - 2)
                    query_part((j - 2) * 2, 2)

    for r in range(4):
        if r < 3:
            step(wide(BLOCKS - 1), r + 4)
        step(tail(0), r)
        if r < 2:
            anchor_step(4 * BLOCKS + r - 8)
        if r == 3:
            project_pair(2)
            query_part(4, 2)
        else:

            @pl.loop(0, 2)
            def _(hh):
                if r > 0:
                    attend((r - 1) * 2 + hh)

    for r in range(4):
        if r < 3:
            step(tail(0), r + 4)
        step(tail(1), r)
        if r < 2:
            attend(4 + r)
        if r == 3:
            project(w_tail.at[0], 0, ROWS, HEAD)
            keep_block(6, 0)
            keep_query(6, 0)
            query_part(6, 1)
    for r in range(3):
        step(tail(1), r + 4)
        if r == 0:
            attend(6)
    project(w_tail.at[1], BLK, QT, HEAD)
    keep_query(7, 0)
    query_part(7, 1)
    project(w_tail.at[1], 0, BLK, HEAD)
    keep_block(7, 0)

    @pl.loop(0, N_CTX)
    def _(n):
        @pl.when(n != c)
        def _():
            piece = parts.at[n]
            pltpu.make_async_remote_copy(
                src_ref=piece, dst_ref=piece, send_sem=p_send.at[n], recv_sem=p_recv.at[n],
                device_id=(n, t), device_id_type=MESH,
            ).wait_recv()

    peaks = parts[:, :, HEAD : HEAD + 1]
    top = jnp.max(peaks, 0)
    scaled = jnp.exp2((peaks - top[None]) * POWER)
    total_all = jnp.sum(parts[:, :, HEAD + HEAD // 2 : HEAD + HEAD // 2 + 1] * scaled, 0)
    mixed_all = jnp.sum(parts[:, :, :HEAD] * scaled, 0)

    first = lax.rem(c, QT // OWN) * OWN
    mine = qq_s[pl.ds(pl.multiple_of(c * OWN, OWN), OWN), :]
    scores = dot_nt(mine, kv[BLK:, :HEAD])
    row = lax.broadcasted_iota(jnp.int32, scores.shape, 0) + first
    scores = jnp.where(row >= lax.broadcasted_iota(jnp.int32, scores.shape, 1), scores, NEG)
    peak = jnp.max(scores, 1, keepdims=True)
    weights = jnp.exp2((scores - peak) * POWER)
    total = jnp.sum(weights, 1, keepdims=True)
    mixed = jnp.dot(weights.astype(BF16), kv[BLK:, HEAD:], preferred_element_type=F32)
    final = jnp.maximum(top, peak)
    w_ctx = jnp.exp2((top - final) * POWER)
    w_self = jnp.exp2((peak - final) * POWER)
    done = (mixed_all * w_ctx + mixed * w_self) / (total_all * w_ctx + total * w_self)

    def result_at(n):
        return qout_ref.at[
            pl.ds(pl.multiple_of(lax.rem(n, QT // OWN) * OWN, OWN), OWN),
            pl.ds(pl.multiple_of(lax.div(n, QT // OWN) * HEAD, HEAD), HEAD),
        ]

    def result_copy(source, target):
        piece = result_at(source)
        return pltpu.make_async_remote_copy(
            src_ref=piece, dst_ref=piece, send_sem=r_send.at[target], recv_sem=r_recv.at[source],
            device_id=(target, t), device_id_type=MESH,
        )

    result_at(c)[...] = done.astype(BF16)

    @pl.loop(1, N_CTX)
    def _(d):
        result_copy(c, lax.rem(c + d, N_CTX)).start()

    attend(7)

    @pl.loop(1, N_CTX)
    def _(d):
        other = lax.rem(c + d, N_CTX)
        result_copy(other, other).wait_recv()

    @pl.loop(1, N_CTX)
    def _(d):
        other = lax.rem(c + d, N_CTX)
        result_copy(c, other).wait_send()
        send_part(other).wait_send()

    def w_end(blk):
        for line in range(4):
            rows = (3 * CUT // 2 + 8 * (3 * REST // 2)) if line < 2 else 7 * REST // 2 + 4 * (7 * CUT // 2)
            w_copy(blk, pl.ds(0, rows), ctx_at(1, 0), line, 0).wait_send()

    @pl.loop(0, BLOCKS)
    def _(b):
        w_end(wide(b))

    for b in range(TAILS):
        w_end(tail(b))

    for way in (0, 1):
        for chunk in range(4):
            x_near(way, chunk, 0).wait_send()
        for chunk in FAR[way]:
            x_far(way, chunk, 0).wait_send()
    for dx in (0, 1, -1, 2):
        x_across(dx).wait_send()
    anchor_end()


def on_device(rows, query_rows, positions, bound, wq, wk, wv):
    freq = np.asarray(rope_table(HEAD // 2) * 2, np.float32)[None]
    anywhere = pl.BlockSpec(memory_space=pl.ANY)
    vmem = pl.BlockSpec(memory_space=pltpu.VMEM)
    dma = pltpu.SemaphoreType.DMA
    return pl.pallas_call(
        kernel,
        out_shape=(
            jax.ShapeDtypeStruct((BLK, 8 * HEAD), BF16),
            jax.ShapeDtypeStruct((QT, 8 * HEAD), BF16),
        ),
        in_specs=[anywhere] * 5 + [vmem] * 3,
        out_specs=(vmem, vmem),
        scratch_shapes=[
            pltpu.VMEM((BLOCKS, N_CTX * SHARD, COLS), BF16),
            pltpu.VMEM((TAILS, N_CTX * SHARD, HEAD), BF16),
            pltpu.VMEM((8, ROWS, FEATS), BF16),
            pltpu.VMEM((ROWS, HEAD), F32),
            pltpu.VMEM((ROWS, HEAD), F32),
            pltpu.VMEM((ROWS, COLS), F32),
            pltpu.VMEM((ROWS, COLS), BF16),
            pltpu.VMEM((BLK, COLS), BF16),
            pltpu.VMEM((8, BLK, HEAD), BF16),
            pltpu.VMEM((8 * QT, HEAD), BF16),
            pltpu.VMEM((8 * QT, 2 * HEAD), F32),
            pltpu.VMEM((N_CTX, OWN, 2 * HEAD), F32),
            dma((3 + BLOCKS + TAILS,)),
            dma((BLOCKS + TAILS, 4)),
            dma((BLOCKS + TAILS, PLACES)),
            dma((3, 4)),
            dma((3, 4)),
            dma((4,)),
            dma((4,)),
            dma((4,)),
            dma((4,)),
            dma((N_CTX,)),
            dma((N_CTX,)),
            dma((N_CTX,)),
            dma((N_CTX,)),
        ],
        compiler_params=pltpu.CompilerParams(
            collective_id=0, has_side_effects=True, vmem_limit_bytes=56 << 20
        ),
        name="star_prefill",
    )(rows, query_rows, wq, wk, wv, positions[None], bound[None], freq)


def solution(mesh):
    placed = (
        P("ctx", "tp"),
        P(None, "tp"),
        P(),
        P(),
        P("ctx", "tp"),
        P("ctx", "tp"),
        P("ctx", "tp"),
    )
    return jax.shard_map(
        on_device,
        mesh=mesh,
        in_specs=placed,
        out_specs=(P("ctx", "tp"), P(None, "tp")),
        check_vma=False,
    )
```

```python
import math

import jax
import jax.numpy as jnp
import numpy as np
from jax import lax
from jax.experimental import pallas as pl
from jax.experimental.pallas import tpu as pltpu
from jax.sharding import PartitionSpec as P

MESH = pl.DeviceIdType.MESH
HEAD = 128
NX, NY, NZ = 4, 4, 8
N_CTX = NY * NZ
BLK = 512
QT = 64
ROWS = BLK + QT
SHARD = 256
CUT = 96
REST = SHARD - CUT
BLOCKS = 5
COLS = 256
CHUNK = ROWS // 4
FEATS = 1024
NEG = -1e30
POWER = math.log2(math.e) / math.sqrt(HEAD)
OWN = BLK // N_CTX
F32, BF16 = jnp.float32, jnp.bfloat16


def rope_table(half):
    values = []
    for index in range(half):
        freq = 500000.0 ** (-2.0 * index / (2.0 * half))
        wavelen = 2.0 * math.pi / freq
        if wavelen > 8192.0:
            values.append(freq / 8.0)
        elif wavelen < 2048.0:
            values.append(freq)
        else:
            smooth = (8192.0 / wavelen - 1.0) / 3.0
            values.append((1.0 - smooth) * freq / 8.0 + smooth * freq)
    return values


def bz_at(way, dist):
    return way * 4 + dist - 1


def by_at(off, way, stage):
    return 8 + (off % NZ) * 4 + way * 2 + stage - 1


def ay_at(way, stage):
    return 40 + way * 2 + stage - 1


def az_at(off, way, dist):
    return 44 + (off % NY) * 8 + way * 4 + dist - 1


PLACES = 76
SIGN = (1, -1)


def column(row):
    n = row.shape[1]
    same = lax.broadcasted_iota(jnp.int32, (n, n), 0) == lax.broadcasted_iota(jnp.int32, (n, n), 1)
    return jnp.sum(jnp.where(same, jnp.broadcast_to(row, (n, n)), 0.0), axis=1, keepdims=True)


def dot_nt(a, b):
    return lax.dot_general(a, b, (((1,), (1,)), ((), ())), preferred_element_type=F32)


def kernel(
    x_ref, xq_ref, wq_ref, wk_ref, wv_ref, pos_ref, bound_ref, freq_ref,
    out_ref, qout_ref,
    w_all, x_all, cos_s, sin_s, acc, kv, akv, q_s, qq_s, terms, term_in, part, parts,
    local_sem, w_send, w_recv, x_send, x_recv, sib_send, sib_recv, a_send, a_recv,
    t_send, t_recv, q_send, q_recv, p_send, p_recv, r_send, r_recv,
):
    c = lax.axis_index("ctx")
    t = lax.axis_index("tp")
    y, z = lax.div(c, NZ), lax.rem(c, NZ)
    x, core = lax.div(t, 2), lax.rem(t, 2)

    def ctx_at(dy, dz):
        return lax.rem(y + dy + NY, NY) * NZ + lax.rem(z + dz + NZ, NZ)

    def tp_at(dx):
        return lax.rem(x + dx + NX, NX) * 2 + core

    sibling = x * 2 + 1 - core

    locals_ = [
        pltpu.make_async_copy(x_ref, x_all.at[t, pl.ds(0, BLK)], local_sem.at[0]),
        pltpu.make_async_copy(xq_ref, x_all.at[t, pl.ds(BLK, QT)], local_sem.at[1]),
    ]
    own = pl.ds(pl.multiple_of(c * SHARD, SHARD), SHARD)
    locals_.append(pltpu.make_async_copy(wk_ref, w_all.at[0, own, pl.ds(0, HEAD)], local_sem.at[2]))
    locals_.append(pltpu.make_async_copy(wv_ref, w_all.at[0, own, pl.ds(HEAD, HEAD)], local_sem.at[3]))
    for b in range(1, BLOCKS):
        locals_.append(
            pltpu.make_async_copy(
                wq_ref.at[:, pl.ds((b - 1) * COLS, COLS)], w_all.at[b, own], local_sem.at[3 + b]
            )
        )
    for copy in locals_:
        copy.start()

    barrier = pltpu.get_barrier_semaphore()

    @pl.loop(1, N_CTX)
    def _(d):
        pl.semaphore_signal(barrier, inc=1, device_id=(lax.rem(c + d, N_CTX), t), device_id_type=MESH)

    for other in (tp_at(1), tp_at(-1), sibling):
        pl.semaphore_signal(barrier, inc=1, device_id=(c, other), device_id_type=MESH)
    pl.semaphore_wait(barrier, N_CTX - 1 + 3)
    for copy in locals_:
        copy.wait()

    def rows_of(origin, first, count, dist, full, way):
        if dist == full:
            half = count // 2
            first, count = first + (half if way else 0), half
        return pl.ds(pl.multiple_of(origin * SHARD + first, 16), count)

    def w_copy(b, rows, target, line, place):
        piece = w_all.at[b, rows]
        return pltpu.make_async_remote_copy(
            src_ref=piece, dst_ref=piece, send_sem=w_send.at[b, line], recv_sem=w_recv.at[b, place],
            device_id=(target, t), device_id_type=MESH,
        )

    def bz(b, way, dist, hop):
        s = SIGN[way]
        rows = rows_of(ctx_at(0, -s * (dist - 1 + hop)), CUT, REST, dist, 4, way)
        return w_copy(b, rows, ctx_at(0, s), 2 + way, bz_at(way, dist))

    def by(b, off, way, stage, hop):
        s = SIGN[way]
        rows = rows_of(ctx_at(-s * (stage - 1 + hop), off), CUT, REST, stage, 2, way)
        return w_copy(b, rows, ctx_at(s, 0), way, by_at(off, way, stage))

    def ay(b, way, stage, hop):
        s = SIGN[way]
        rows = rows_of(ctx_at(-s * (stage - 1 + hop), 0), 0, CUT, stage, 2, way)
        return w_copy(b, rows, ctx_at(s, 0), way, ay_at(way, stage))

    def az(b, off, way, dist, hop):
        s = SIGN[way]
        rows = rows_of(ctx_at(off, -s * (dist - 1 + hop)), 0, CUT, dist, 4, way)
        return w_copy(b, rows, ctx_at(0, s), 2 + way, az_at(off, way, dist))

    def go(make, *args):
        make(*args, 0).start()

    def got(make, *args):
        make(*args, 1).wait_recv()

    def step(b, s):
        if s == 0:
            for way in (0, 1):
                go(bz, b, way, 1)
                go(ay, b, way, 1)
            for way in (0, 1):
                go(az, b, 0, way, 1)
                go(by, b, 0, way, 1)
            return
        if s <= 4:
            for way in (0, 1):
                got(bz, b, way, s)
                if s < 4:
                    go(bz, b, way, s + 1)
                    go(by, b, -SIGN[way] * s, 0, 1)
                    go(by, b, -SIGN[way] * s, 1, 1)
            if s == 4:
                go(by, b, 4, 0, 1)
                go(by, b, 4, 1, 1)
        if s == 1:
            for way in (0, 1):
                got(ay, b, way, 1)
                go(ay, b, way, 2)
                go(az, b, -SIGN[way], 0, 1)
                go(az, b, -SIGN[way], 1, 1)
        if s == 2:
            got(ay, b, 0, 2)
            got(ay, b, 1, 2)
            go(az, b, 2, 0, 1)
            go(az, b, 2, 1, 1)
        for off, since in ((0, 0), (1, 1), (-1, 1), (2, 2)):
            dist = s - since
            if 1 <= dist <= 4:
                for way in (0, 1):
                    got(az, b, off, way, dist)
                    if dist < 4:
                        go(az, b, off, way, dist + 1)
        for group in range(5):
            offs = (0,) if group == 0 else (4,) if group == 4 else (-group, group)
            stage = s - group
            if 1 <= stage <= 2:
                for off in offs:
                    for way in (0, 1):
                        got(by, b, off, way, stage)
                        if stage == 1:
                            go(by, b, off, way, 2)

    def x_copy(dx, rows, target, send, recv):
        piece = x_all.at[tp_at(dx), rows]
        return pltpu.make_async_remote_copy(
            src_ref=piece, dst_ref=piece, send_sem=send, recv_sem=recv,
            device_id=(c, target), device_id_type=MESH,
        )

    def x_near(way, chunk, hop):
        return x_copy(-SIGN[way] * hop, pl.ds(chunk * CHUNK, CHUNK), tp_at(SIGN[way]), x_send.at[way, chunk], x_recv.at[way, chunk])

    def x_far(way, chunk, hop):
        return x_copy(-SIGN[way] * (1 + hop), pl.ds(chunk * CHUNK, CHUNK), tp_at(SIGN[way]), x_send.at[2, chunk], x_recv.at[2, chunk])

    FAR = ((0, 1), (2, 3))

    def x_across(dx):
        piece = x_all.at[tp_at(dx)]
        return pltpu.make_async_remote_copy(
            src_ref=piece, dst_ref=piece, send_sem=sib_send.at[dx % 4], recv_sem=sib_recv.at[dx % 4],
            device_id=(c, sibling), device_id_type=MESH,
        )

    def x_arrives(dx):
        piece = x_all.at[lax.rem(x + dx + NX, NX) * 2 + 1 - core]
        return pltpu.make_async_remote_copy(
            src_ref=piece, dst_ref=piece, send_sem=sib_send.at[dx % 4], recv_sem=sib_recv.at[dx % 4],
            device_id=(c, sibling), device_id_type=MESH,
        )

    def x_first():
        for way in (0, 1):
            for chunk in FAR[way] + FAR[1 - way]:
                x_near(way, chunk, 0).start()
        x_across(0).start()

    def x_second():
        for way in (0, 1):
            for chunk in FAR[way]:
                x_near(way, chunk, 1).wait_recv()
                x_far(way, chunk, 0).start()

    def x_third():
        for way in (0, 1):
            for chunk in FAR[1 - way]:
                x_near(way, chunk, 1).wait_recv()
            x_across(-SIGN[way]).start()

    def x_fourth():
        for way in (0, 1):
            for chunk in FAR[way]:
                x_far(way, chunk, 1).wait_recv()
        x_across(2).start()

    def x_last():
        for dx in (0, 1, -1, 2):
            x_arrives(dx).wait_recv()

    def angles(first, positions):
        angle = positions * freq_ref[...]
        lane = lax.broadcasted_iota(jnp.int32, angle.shape, 1)
        cosine, sine = jnp.cos(angle), jnp.sin(angle)
        rows = pl.ds(first, angle.shape[0])
        cos_s[rows, :] = cosine
        sin_s[rows, :] = jnp.where(lane < HEAD // 2, -sine, sine)

    def block_angles(first, count):
        place = lax.broadcasted_iota(jnp.int32, (count, HEAD), 0) + (c * BLK + first)
        angles(first, place.astype(F32))

    def query_angles():
        place = column(pos_ref[...].astype(F32))
        angles(BLK, jnp.broadcast_to(place, (QT, HEAD)))

    def project(weights, first, count, columns):
        acc[first : first + count, :columns] = jnp.zeros((count, columns), F32)

        @pl.loop(0, 8)
        def _(s):
            acc[first : first + count, :columns] += jnp.dot(
                x_all[s, first : first + count],
                weights[pl.ds(pl.multiple_of(s * FEATS, FEATS), FEATS), :],
                preferred_element_type=F32,
            )

    def rotate(first, count, lane):
        u = acc[first : first + count, lane : lane + HEAD]
        turned = u * cos_s[first : first + count] + pltpu.roll(u, HEAD // 2, 1) * sin_s[first : first + count]
        return turned.astype(BF16)

    def project_kv():
        project(w_all.at[0], 0, ROWS, COLS)
        kv[:, :HEAD] = rotate(0, ROWS, 0)
        kv[:, HEAD:] = acc[:, HEAD:].astype(BF16)

    def keep_block(head, lane):
        q_s[head] = rotate(0, BLK, lane)

    def project_pair(pair):
        project(w_all.at[pair + 1], 0, BLK, COLS)
        for hh in range(2):
            keep_block(pair * 2 + hh, hh * HEAD)

    def others(act):
        @pl.loop(1, N_CTX)
        def _(d):
            act(lax.rem(c + d, N_CTX))

    def own_rows(n):
        return pl.ds(pl.multiple_of(n * OWN, OWN), OWN)

    def exchange(source, target, sems, slot, peer):
        return pltpu.make_async_remote_copy(
            src_ref=source, dst_ref=target, send_sem=sems[0].at[peer], recv_sem=sems[1].at[slot],
            device_id=(peer, t), device_id_type=MESH,
        )

    def term_to(n):
        return exchange(terms.at[own_rows(n)], term_in.at[c], (t_send, t_recv), c, n)

    def term_from(n):
        return exchange(terms.at[own_rows(n)], term_in.at[n], (t_send, t_recv), n, n)

    def qq_to(n):
        return exchange(qq_s.at[own_rows(c)], qq_s.at[own_rows(c)], (q_send, q_recv), c, n)

    def qq_from(n):
        return exchange(qq_s.at[own_rows(n)], qq_s.at[own_rows(n)], (q_send, q_recv), n, n)

    def part_to(n):
        return exchange(part.at[n], parts.at[c], (p_send, p_recv), c, n)

    def part_from(n):
        return exchange(part.at[n], parts.at[n], (p_send, p_recv), n, n)

    def query_terms():
        share = x_all[lax.div(c, 4), BLK:, pl.ds(pl.multiple_of(lax.rem(c, 4) * SHARD, SHARD), SHARD)]
        for pair in range(4):
            term = jnp.dot(share, w_all[pair + 1, own, :], preferred_element_type=F32)
            terms[pair * 2 * QT : (pair * 2 + 1) * QT, :] = term[:, :HEAD]
            terms[(pair * 2 + 1) * QT : (pair * 2 + 2) * QT, :] = term[:, HEAD:]
        term_in[c] = terms[own_rows(c), :]
        others(lambda n: term_to(n).start())

    def query_sum():
        others(lambda n: term_from(n).wait_recv())
        u = jnp.sum(term_in[...], 0)
        place = pl.ds(pl.multiple_of(BLK + lax.rem(c, QT // OWN) * OWN, OWN), OWN)
        turned = u * cos_s[place, :] + pltpu.roll(u, HEAD // 2, 1) * sin_s[place, :]
        qq_s[own_rows(c), :] = turned.astype(BF16)
        others(lambda n: qq_to(n).start())

    def query_part():
        others(lambda n: qq_from(n).wait_recv())
        bound = column(bound_ref[...].astype(F32))
        bound = jnp.concatenate([bound] * 2, 0)

        @pl.loop(0, 4)
        def _(pair):
            rows = pl.ds(pl.multiple_of(pair * 2 * QT, 2 * QT), 2 * QT)
            scores = dot_nt(qq_s[rows, :], kv[:BLK, :HEAD])
            place = (lax.broadcasted_iota(jnp.int32, scores.shape, 1) + c * BLK).astype(F32)
            scores = jnp.where(place < bound, scores, NEG)
            peak = jnp.max(scores, 1, keepdims=True)
            weights = jnp.exp2((scores - peak) * POWER)
            total = jnp.sum(weights, 1, keepdims=True)
            mixed = jnp.dot(weights.astype(BF16), kv[:BLK, HEAD:], preferred_element_type=F32)
            lane = lax.broadcasted_iota(jnp.int32, (8, HEAD), 1)
            for n in range(8):
                first = n * OWN
                part[pair * 8 + n, :OWN, :] = mixed[first : first + OWN]
                peak_0, peak_1 = peak[first : first + 8], peak[first + 8 : first + 16]
                total_0, total_1 = total[first : first + 8], total[first + 8 : first + 16]
                part[pair * 8 + n, OWN:, :] = jnp.where(
                    lane < 2,
                    jnp.where(lane == 0, peak_0, peak_1),
                    jnp.where(lane == 2, total_0, total_1),
                )

        parts[c] = part[c]
        others(lambda n: part_to(n).start())

    def result_at(n):
        return qout_ref.at[
            pl.ds(pl.multiple_of(lax.rem(n, QT // OWN) * OWN, OWN), OWN),
            pl.ds(pl.multiple_of(lax.div(n, QT // OWN) * HEAD, HEAD), HEAD),
        ]

    def result_copy(source, target):
        piece = result_at(source)
        return exchange(piece, piece, (r_send, r_recv), source, target)

    def query_merge():
        others(lambda n: part_from(n).wait_recv())

        def halves(lane):
            return jnp.concatenate(
                [parts[:, OWN:, lane : lane + 1], parts[:, OWN:, lane + 1 : lane + 2]], 1
            )

        peaks = halves(0)
        top = jnp.max(peaks, 0)
        scaled = jnp.exp2((peaks - top[None]) * POWER)
        total_all = jnp.sum(halves(2) * scaled, 0)
        mixed_all = jnp.sum(parts[:, :OWN, :] * scaled, 0)

        first = lax.rem(c, QT // OWN) * OWN
        scores = dot_nt(qq_s[own_rows(c), :], kv[BLK:, :HEAD])
        row = lax.broadcasted_iota(jnp.int32, scores.shape, 0) + first
        scores = jnp.where(row >= lax.broadcasted_iota(jnp.int32, scores.shape, 1), scores, NEG)
        peak = jnp.max(scores, 1, keepdims=True)
        weights = jnp.exp2((scores - peak) * POWER)
        total = jnp.sum(weights, 1, keepdims=True)
        mixed = jnp.dot(weights.astype(BF16), kv[BLK:, HEAD:], preferred_element_type=F32)
        final = jnp.maximum(top, peak)
        w_ctx = jnp.exp2((top - final) * POWER)
        w_self = jnp.exp2((peak - final) * POWER)
        done = (mixed_all * w_ctx + mixed * w_self) / (total_all * w_ctx + total * w_self)
        result_at(c)[...] = done.astype(BF16)
        others(lambda n: result_copy(c, n).start())

    def attend(head):
        bias = jnp.where(c > 0, 0.0, NEG).astype(F32)
        tile = BLK // 2
        for n in range(2):
            span = (n + 1) * tile
            q = q_s[head, n * tile : span, :]
            far = dot_nt(q, akv[:, :HEAD])
            near = dot_nt(q, kv[:span, :HEAD])
            row = lax.broadcasted_iota(jnp.int32, near.shape, 0) + n * tile
            near = jnp.where(row >= lax.broadcasted_iota(jnp.int32, near.shape, 1), near, NEG)
            peak = jnp.maximum(
                jnp.max(far, 1, keepdims=True) + bias, jnp.max(near, 1, keepdims=True)
            )
            far = jnp.exp2((far - (peak - bias)) * POWER)
            near = jnp.exp2((near - peak) * POWER)
            total = jnp.sum(far, 1, keepdims=True) + jnp.sum(near, 1, keepdims=True)
            mixed = jnp.dot(far.astype(BF16), akv[:, HEAD:], preferred_element_type=F32)
            mixed += jnp.dot(near.astype(BF16), kv[:span, HEAD:], preferred_element_type=F32)
            out_ref[n * tile : span, pl.ds(pl.multiple_of(head * HEAD, HEAD), HEAD)] = (
                mixed / total
            ).astype(BF16)

    def attend_pair(pair):
        @pl.loop(0, 2)
        def _(hh):
            attend(pair * 2 + hh)

    depth = jnp.where(y == 3, 1, y) + jnp.minimum(z, NZ - z)

    def anchor_copy(first, count, target, line, place):
        piece = akv.at[pl.ds(first, count)]
        return pltpu.make_async_remote_copy(
            src_ref=piece, dst_ref=piece, send_sem=a_send.at[line], recv_sem=a_recv.at[place],
            device_id=(target, t), device_id_type=MESH,
        )

    PIECE = BLK // 4
    HALF = BLK // 2

    def anchor_lines(act):
        @pl.when((z == 0) & (y < 2))
        def _():
            act(ctx_at(1, 0), 0)

        @pl.when(c == 0)
        def _():
            act(ctx_at(-1, 0), 1)

        @pl.when(z < 3)
        def _():
            act(ctx_at(0, 1), 2)

        @pl.when((z > 5) | (z == 0))
        def _():
            act(ctx_at(0, -1), 3)

    def anchor_piece(k, target, line):
        return anchor_copy(pl.multiple_of(k * PIECE, PIECE), PIECE, target, line, k)

    def anchor_step(g):
        k = g - depth

        @pl.when((k >= 0) & (k < 4))
        def _():
            @pl.when(depth > 0)
            def _():
                anchor_piece(k, ctx_at(0, 1), 2).wait_recv()

            anchor_lines(lambda target, line: anchor_piece(k, target, line).start())

            @pl.when((z == 3) & (k < 2))
            def _():
                anchor_piece(k, ctx_at(0, 1), 2).start()

            @pl.when((z == 5) & (k >= 2))
            def _():
                anchor_piece(k, ctx_at(0, -1), 3).start()

    def anchor_root():
        @pl.when(c == 0)
        def _():
            akv[...] = kv[:BLK, :]

    def anchor_end():
        anchor_lines(lambda target, line: anchor_copy(0, BLK, target, line, 0).wait_send())

        @pl.when(z == 3)
        def _():
            anchor_copy(0, HALF, ctx_at(0, 1), 2, 0).wait_send()

        @pl.when(z == 5)
        def _():
            anchor_copy(0, HALF, ctx_at(0, -1), 3, 0).wait_send()

    x_first()

    @pl.loop(0, BLOCKS + 1)
    def _(j):
        for r in range(4):

            def at(n, *acts):
                @pl.when(j == n)
                def _():
                    for act in acts:
                        act()

            if r < 3:

                @pl.when(j >= 1)
                def _():
                    step(j - 1, r + 4)

            @pl.when(j < BLOCKS)
            def _():
                step(j, r)

            if r == 0:
                at(2, x_last, project_kv, anchor_root)

            anchor_step(4 * j + r - 8)

            at(0, lambda: block_angles(r * (BLK // 4), BLK // 4))
            if r == 0:
                at(5, lambda: attend_pair(1))
            if r == 1:
                at(1, x_third)
                at(2, query_terms)
                at(4, query_merge)
                at(5, lambda: attend_pair(2))
            if r == 2:
                at(3, query_part)
                at(4, lambda: attend_pair(0))
            if r == 3:
                at(0, query_angles, x_second)
                at(1, x_fourth)
                at(2, query_sum)

                @pl.when(j >= 2)
                def _():
                    project_pair(j - 2)

    attend_pair(3)
    others(lambda n: result_copy(n, n).wait_recv())

    def left(n):
        term_to(n).wait_send()
        qq_to(n).wait_send()
        part_to(n).wait_send()
        result_copy(c, n).wait_send()

    others(left)

    @pl.loop(0, BLOCKS)
    def _(b):
        for line in range(4):
            rows = (3 * CUT // 2 + 8 * (3 * REST // 2)) if line < 2 else 7 * REST // 2 + 4 * (7 * CUT // 2)
            w_copy(b, pl.ds(0, rows), ctx_at(1, 0), line, 0).wait_send()

    for way in (0, 1):
        for chunk in range(4):
            x_near(way, chunk, 0).wait_send()
        for chunk in FAR[way]:
            x_far(way, chunk, 0).wait_send()
    for dx in (0, 1, -1, 2):
        x_across(dx).wait_send()
    anchor_end()


def on_device(rows, query_rows, positions, bound, wq, wk, wv):
    freq = np.asarray(rope_table(HEAD // 2) * 2, np.float32)[None]
    anywhere = pl.BlockSpec(memory_space=pl.ANY)
    vmem = pl.BlockSpec(memory_space=pltpu.VMEM)
    dma = pltpu.SemaphoreType.DMA
    return pl.pallas_call(
        kernel,
        out_shape=(
            jax.ShapeDtypeStruct((BLK, 8 * HEAD), BF16),
            jax.ShapeDtypeStruct((QT, 8 * HEAD), BF16),
        ),
        in_specs=[anywhere] * 5 + [vmem] * 3,
        out_specs=(vmem, vmem),
        scratch_shapes=[
            pltpu.VMEM((BLOCKS, N_CTX * SHARD, COLS), BF16),
            pltpu.VMEM((8, ROWS, FEATS), BF16),
            pltpu.VMEM((ROWS, HEAD), F32),
            pltpu.VMEM((ROWS, HEAD), F32),
            pltpu.VMEM((ROWS, COLS), F32),
            pltpu.VMEM((ROWS, COLS), BF16),
            pltpu.VMEM((BLK, COLS), BF16),
            pltpu.VMEM((8, BLK, HEAD), BF16),
            pltpu.VMEM((8 * QT, HEAD), BF16),
            pltpu.VMEM((8 * QT, HEAD), F32),
            pltpu.VMEM((N_CTX, OWN, HEAD), F32),
            pltpu.VMEM((N_CTX, OWN + 8, HEAD), F32),
            pltpu.VMEM((N_CTX, OWN + 8, HEAD), F32),
            dma((3 + BLOCKS,)),
            dma((BLOCKS, 4)),
            dma((BLOCKS, PLACES)),
            dma((3, 4)),
            dma((3, 4)),
            dma((4,)),
            dma((4,)),
            dma((4,)),
            dma((4,)),
            dma((N_CTX,)),
            dma((N_CTX,)),
            dma((N_CTX,)),
            dma((N_CTX,)),
            dma((N_CTX,)),
            dma((N_CTX,)),
            dma((N_CTX,)),
            dma((N_CTX,)),
        ],
        compiler_params=pltpu.CompilerParams(
            collective_id=0, has_side_effects=True, vmem_limit_bytes=56 << 20
        ),
        name="star_prefill",
    )(rows, query_rows, wq, wk, wv, positions[None], bound[None], freq)


def solution(mesh):
    placed = (
        P("ctx", "tp"),
        P(None, "tp"),
        P(),
        P(),
        P("ctx", "tp"),
        P("ctx", "tp"),
        P("ctx", "tp"),
    )
    return jax.shard_map(
        on_device,
        mesh=mesh,
        in_specs=placed,
        out_specs=(P("ctx", "tp"), P(None, "tp")),
        check_vma=False,
    )
```

```python
import math

import jax
import jax.numpy as jnp
import numpy as np
from jax import lax
from jax.experimental import pallas as pl
from jax.experimental.pallas import tpu as pltpu
from jax.sharding import PartitionSpec as P

MESH = pl.DeviceIdType.MESH
HEAD = 128
NX, NY, NZ = 4, 4, 8
N_CTX = NY * NZ
BLK = 512
QT = 64
ROWS = BLK + QT
SHARD = 256
CUT = 96
REST = SHARD - CUT
BLOCKS = 5
COLS = 256
CHUNK = ROWS // 4
FEATS = 1024
STAGGER = 3
LAG = 2
ANCHOR_SLOT = 7
NEG = -1e30
POWER = math.log2(math.e) / math.sqrt(HEAD)
OWN = BLK // N_CTX
F32, BF16 = jnp.float32, jnp.bfloat16


def rope_table(half):
    values = []
    for index in range(half):
        freq = 500000.0 ** (-2.0 * index / (2.0 * half))
        wavelen = 2.0 * math.pi / freq
        if wavelen > 8192.0:
            values.append(freq / 8.0)
        elif wavelen < 2048.0:
            values.append(freq)
        else:
            smooth = (8192.0 / wavelen - 1.0) / 3.0
            values.append((1.0 - smooth) * freq / 8.0 + smooth * freq)
    return values


def bz_at(dist):
    return dist - 1


def by_at(off, stage):
    return 4 + (off % NZ) * 2 + stage - 1


def ay_at(stage):
    return 20 + stage - 1


def az_at(off, dist):
    return 22 + (off % NY) * 4 + dist - 1


PLACES = 38
SIGN = (1, -1)


def column(row):
    n = row.shape[1]
    same = lax.broadcasted_iota(jnp.int32, (n, n), 0) == lax.broadcasted_iota(jnp.int32, (n, n), 1)
    return jnp.sum(jnp.where(same, jnp.broadcast_to(row, (n, n)), 0.0), axis=1, keepdims=True)


def dot_nt(a, b):
    return lax.dot_general(a, b, (((1,), (1,)), ((), ())), preferred_element_type=F32)


def kernel(
    x_ref, xq_ref, wq_ref, wk_ref, wv_ref, pos_ref, bound_ref, freq_ref,
    out_ref, qout_ref,
    w_all, x_all, cos_s, sin_s, acc, kv, akv, q_s, qq_s, terms, term_in, mixed_out, mixed_in, level_out, level_in,
    local_sem, w_send, w_recv, x_send, x_recv, sib_send, sib_recv, a_send, a_recv,
    ex_send, ex_recv,
):
    c = lax.axis_index("ctx")
    t = lax.axis_index("tp")
    y, z = lax.div(c, NZ), lax.rem(c, NZ)
    x, core = lax.div(t, 2), lax.rem(t, 2)

    def ctx_at(dy, dz):
        return lax.rem(y + dy + NY, NY) * NZ + lax.rem(z + dz + NZ, NZ)

    def tp_at(dx):
        return lax.rem(x + dx + NX, NX) * 2 + core

    sibling = x * 2 + 1 - core

    locals_ = [
        pltpu.make_async_copy(x_ref, x_all.at[t, pl.ds(0, BLK)], local_sem.at[0]),
        pltpu.make_async_copy(xq_ref, x_all.at[t, pl.ds(BLK, QT)], local_sem.at[1]),
    ]
    own = pl.ds(pl.multiple_of(c * SHARD, SHARD), SHARD)
    locals_.append(pltpu.make_async_copy(wk_ref, w_all.at[0, own, pl.ds(0, HEAD)], local_sem.at[2]))
    locals_.append(pltpu.make_async_copy(wv_ref, w_all.at[0, own, pl.ds(HEAD, HEAD)], local_sem.at[3]))
    for b in range(1, BLOCKS):
        locals_.append(
            pltpu.make_async_copy(
                wq_ref.at[:, pl.ds((b - 1) * COLS, COLS)], w_all.at[b, own], local_sem.at[3 + b]
            )
        )
    for copy in locals_:
        copy.start()

    barrier = pltpu.get_barrier_semaphore()

    @pl.loop(1, N_CTX)
    def _(d):
        pl.semaphore_signal(barrier, inc=1, device_id=(lax.rem(c + d, N_CTX), t), device_id_type=MESH)

    for other in (tp_at(1), tp_at(-1), sibling):
        pl.semaphore_signal(barrier, inc=1, device_id=(c, other), device_id_type=MESH)
    pl.semaphore_wait(barrier, N_CTX - 1 + 3)
    for copy in locals_:
        copy.wait()

    def rows_of(origin, first, count, dist, full, way):
        if dist == full:
            half = count // 2
            first, count = first + (half if way else 0), half
        return pl.ds(pl.multiple_of(origin * SHARD + first, 16), count)

    def w_copy(blk, rows, target, line, place):
        piece = w_all.at[blk, rows]
        return pltpu.make_async_remote_copy(
            src_ref=piece, dst_ref=piece, send_sem=w_send.at[blk, line], recv_sem=w_recv.at[blk, place],
            device_id=(target, t), device_id_type=MESH,
        )

    def bz(blk, way, dist):
        s = SIGN[way]
        rows = rows_of(ctx_at(0, -s * (dist - 1)), CUT, REST, dist, 4, way)
        w_copy(blk, rows, ctx_at(0, s), 2 + way, bz_at(dist)).start()

    def by(blk, off, way, stage):
        s = SIGN[way]
        rows = rows_of(ctx_at(-s * (stage - 1), off), CUT, REST, stage, 2, way)
        w_copy(blk, rows, ctx_at(s, 0), way, by_at(off, stage)).start()

    def ay(blk, way, stage):
        s = SIGN[way]
        rows = rows_of(ctx_at(-s * (stage - 1), 0), 0, CUT, stage, 2, way)
        w_copy(blk, rows, ctx_at(s, 0), way, ay_at(stage)).start()

    def az(blk, off, way, dist):
        s = SIGN[way]
        rows = rows_of(ctx_at(off, -s * (dist - 1)), 0, CUT, dist, 4, way)
        w_copy(blk, rows, ctx_at(0, s), 2 + way, az_at(off, dist)).start()

    def both(make, blk, *args):
        *front, last = args
        for way in (0, 1):
            make(blk, *front, way, last)

    def got(blk, place, count):
        w_copy(blk, pl.ds(0, count), ctx_at(1, 0), 0, place).wait_recv()

    def step(blk, s):
        if s == 0:
            both(bz, blk, 1)
            both(ay, blk, 1)
            both(az, blk, 0, 1)
            both(by, blk, 0, 1)
            return
        if s <= 4:
            got(blk, bz_at(s), 2 * REST if s < 4 else REST)
            if s < 4:
                both(bz, blk, s + 1)
                both(by, blk, -s, 1)
                both(by, blk, s, 1)
            else:
                both(by, blk, 4, 1)
        if s == 1:
            got(blk, ay_at(1), 2 * CUT)
            both(ay, blk, 2)
            both(az, blk, -1, 1)
            both(az, blk, 1, 1)
        if s == 2:
            got(blk, ay_at(2), CUT)
            both(az, blk, 2, 1)
        for off, since in ((0, 0), (1, 1), (-1, 1), (2, 2)):
            dist = s - since
            if 1 <= dist <= 4:
                got(blk, az_at(off, dist), 2 * CUT if dist < 4 else CUT)
                if dist < 4:
                    both(az, blk, off, dist + 1)
        for group in range(5):
            offs = (0,) if group == 0 else (4,) if group == 4 else (-group, group)
            stage = s - group
            if 1 <= stage <= 2:
                for off in offs:
                    got(blk, by_at(off, stage), 2 * REST if stage == 1 else REST)
                    if stage == 1:
                        both(by, blk, off, 2)

    def x_copy(dx, rows, target, send, recv):
        piece = x_all.at[tp_at(dx), rows]
        return pltpu.make_async_remote_copy(
            src_ref=piece, dst_ref=piece, send_sem=send, recv_sem=recv,
            device_id=(c, target), device_id_type=MESH,
        )

    def x_near(way, chunk, hop):
        return x_copy(-SIGN[way] * hop, pl.ds(chunk * CHUNK, CHUNK), tp_at(SIGN[way]), x_send.at[way, chunk], x_recv.at[way, chunk])

    def x_far(way, chunk, hop):
        return x_copy(-SIGN[way] * (1 + hop), pl.ds(chunk * CHUNK, CHUNK), tp_at(SIGN[way]), x_send.at[2, chunk], x_recv.at[2, chunk])

    FAR = ((0, 1), (2, 3))

    def x_across(dx):
        piece = x_all.at[tp_at(dx)]
        return pltpu.make_async_remote_copy(
            src_ref=piece, dst_ref=piece, send_sem=sib_send.at[dx % 4], recv_sem=sib_recv.at[dx % 4],
            device_id=(c, sibling), device_id_type=MESH,
        )

    def x_arrives(dx):
        piece = x_all.at[lax.rem(x + dx + NX, NX) * 2 + 1 - core]
        return pltpu.make_async_remote_copy(
            src_ref=piece, dst_ref=piece, send_sem=sib_send.at[dx % 4], recv_sem=sib_recv.at[dx % 4],
            device_id=(c, sibling), device_id_type=MESH,
        )

    def x_first():
        for way in (0, 1):
            for chunk in FAR[way] + FAR[1 - way]:
                x_near(way, chunk, 0).start()
        x_across(0).start()

    def x_second():
        for way in (0, 1):
            for chunk in FAR[way]:
                x_near(way, chunk, 1).wait_recv()
                x_far(way, chunk, 0).start()

    def x_third():
        for way in (0, 1):
            for chunk in FAR[1 - way]:
                x_near(way, chunk, 1).wait_recv()
            x_across(-SIGN[way]).start()

    def x_fourth():
        for way in (0, 1):
            for chunk in FAR[way]:
                x_far(way, chunk, 1).wait_recv()
        x_across(2).start()

    def x_last():
        for dx in (0, 1, -1, 2):
            x_arrives(dx).wait_recv()

    def angles(first, positions):
        angle = positions * freq_ref[...]
        lane = lax.broadcasted_iota(jnp.int32, angle.shape, 1)
        cosine, sine = jnp.cos(angle), jnp.sin(angle)
        rows = pl.ds(first, angle.shape[0])
        cos_s[rows, :] = cosine
        sin_s[rows, :] = jnp.where(lane < HEAD // 2, -sine, sine)

    def block_angles(first, count):
        place = lax.broadcasted_iota(jnp.int32, (count, HEAD), 0) + (c * BLK + first)
        angles(first, place.astype(F32))

    def query_angles():
        place = column(pos_ref[...].astype(F32))
        angles(BLK, jnp.broadcast_to(place, (QT, HEAD)))

    def add_slice(b, n, rows):
        acc[:rows] += jnp.dot(
            x_all[n, :rows],
            w_all[b, pl.ds(pl.multiple_of(n * FEATS, FEATS), FEATS), :],
            preferred_element_type=F32,
        )

    def project(b, rows):
        acc[...] = jnp.zeros_like(acc)

        @pl.loop(0, 8)
        def _(n):
            add_slice(b, n, rows)

    mine, facing = lax.div(z, 4), 1 - lax.div(z, 4)

    def last_slices(*places):
        for dy, half in places:
            add_slice(BLOCKS - 1, lax.rem(y + dy + NY, NY) * 2 + half, BLK)

    def last_first():
        acc[...] = jnp.zeros_like(acc)
        last_slices((0, mine), (0, facing), (1, mine), (-1, mine))

    def last_second():
        last_slices((1, facing), (-1, facing), (2, mine))

    def last_third():
        last_slices((2, facing))
        for hh in range(2):
            keep_block(6 + hh, hh * HEAD)

    def rotate(first, count, lane):
        u = acc[first : first + count, lane : lane + HEAD]
        turned = u * cos_s[first : first + count] + pltpu.roll(u, HEAD // 2, 1) * sin_s[first : first + count]
        return turned.astype(BF16)

    def project_kv():
        project(0, ROWS)
        kv[:, :HEAD] = rotate(0, ROWS, 0)
        kv[:, HEAD:] = acc[:, HEAD:].astype(BF16)

    def keep_block(head, lane):
        q_s[head] = rotate(0, BLK, lane)

    def project_pair(pair):
        project(pair + 1, BLK)
        for hh in range(2):
            keep_block(pair * 2 + hh, hh * HEAD)

    def others(act):
        @pl.loop(1, N_CTX)
        def _(d):
            act(lax.rem(c + d, N_CTX))

    def own_rows(n):
        return pl.ds(pl.multiple_of(n * OWN, OWN), OWN)

    def exchange(source, target, kind, peer):
        return pltpu.make_async_remote_copy(
            src_ref=source, dst_ref=target, send_sem=ex_send.at[kind], recv_sem=ex_recv.at[kind],
            device_id=(peer, t), device_id_type=MESH,
        )

    def term_to(n):
        return exchange(terms.at[own_rows(n)], term_in.at[c], 0, n)

    def qq_to(n):
        return exchange(qq_s.at[own_rows(c)], qq_s.at[own_rows(c)], 1, n)

    def mixed_to(n):
        return exchange(mixed_out.at[n], mixed_in.at[c], 2, n)

    def level_to(n):
        return exchange(level_out.at[n], level_in.at[c], 3, n)

    def result_to(n):
        return exchange(result_at(c), result_at(c), 4, n)

    def of_all(kind):
        most = pl.ds(0, N_CTX - 1)
        rows = pl.ds(0, (N_CTX - 1) * OWN)
        piece = (term_in.at[most], qq_s.at[rows], mixed_in.at[most], level_in.at[most], qq_s.at[rows])[kind]
        return exchange(piece, piece, kind, ctx_at(1, 0))

    def query_terms():
        share = x_all[lax.div(c, 4), BLK:, pl.ds(pl.multiple_of(lax.rem(c, 4) * SHARD, SHARD), SHARD)]
        for pair in range(4):
            term = jnp.dot(share, w_all[pair + 1, own, :], preferred_element_type=F32)
            terms[pair * 2 * QT : (pair * 2 + 1) * QT, :] = term[:, :HEAD]
            terms[(pair * 2 + 1) * QT : (pair * 2 + 2) * QT, :] = term[:, HEAD:]
        term_in[c] = terms[own_rows(c), :]
        others(lambda n: term_to(n).start())

    def query_sum():
        of_all(0).wait_recv()
        u = jnp.sum(term_in[...], 0)
        place = pl.ds(pl.multiple_of(BLK + lax.rem(c, QT // OWN) * OWN, OWN), OWN)
        turned = u * cos_s[place, :] + pltpu.roll(u, HEAD // 2, 1) * sin_s[place, :]
        qq_s[own_rows(c), :] = turned.astype(BF16)
        others(lambda n: qq_to(n).start())

    def query_part():
        of_all(1).wait_recv()
        bound = column(bound_ref[...].astype(F32))
        bound = jnp.concatenate([bound] * 2, 0)

        @pl.loop(0, 4)
        def _(pair):
            rows = pl.ds(pl.multiple_of(pair * 2 * QT, 2 * QT), 2 * QT)
            scores = dot_nt(qq_s[rows, :], kv[:BLK, :HEAD])
            place = (lax.broadcasted_iota(jnp.int32, scores.shape, 1) + c * BLK).astype(F32)
            scores = jnp.where(place < bound, scores, NEG)
            peak = jnp.max(scores, 1, keepdims=True)
            weights = jnp.exp2((scores - peak) * POWER)
            total = jnp.sum(weights, 1, keepdims=True)
            mixed = jnp.dot(weights.astype(BF16), kv[:BLK, HEAD:], preferred_element_type=F32)
            lane = lax.broadcasted_iota(jnp.int32, (8, HEAD), 1)
            for n in range(8):
                first = n * OWN
                mixed_out[pair * 8 + n] = mixed[first : first + OWN].astype(BF16)
                peak_0, peak_1 = peak[first : first + 8], peak[first + 8 : first + 16]
                total_0, total_1 = total[first : first + 8], total[first + 8 : first + 16]
                level_out[pair * 8 + n] = jnp.where(
                    lane < 2,
                    jnp.where(lane == 0, peak_0, peak_1),
                    jnp.where(lane == 2, total_0, total_1),
                )

        mixed_in[c] = mixed_out[c]
        level_in[c] = level_out[c]

        def both_to(n):
            mixed_to(n).start()
            level_to(n).start()

        others(both_to)

    def result_at(n):
        return qout_ref.at[
            pl.ds(pl.multiple_of(lax.rem(n, QT // OWN) * OWN, OWN), OWN),
            pl.ds(pl.multiple_of(lax.div(n, QT // OWN) * HEAD, HEAD), HEAD),
        ]

    def query_merge():
        of_all(2).wait_recv()
        of_all(3).wait_recv()

        def halves(lane):
            return jnp.concatenate(
                [level_in[:, :, lane : lane + 1], level_in[:, :, lane + 1 : lane + 2]], 1
            )

        peaks = halves(0)
        top = jnp.max(peaks, 0)
        scaled = jnp.exp2((peaks - top[None]) * POWER)
        total_all = jnp.sum(halves(2) * scaled, 0)
        mixed_all = jnp.sum(mixed_in[...].astype(F32) * scaled, 0)

        first = lax.rem(c, QT // OWN) * OWN
        scores = dot_nt(qq_s[own_rows(c), :], kv[BLK:, :HEAD])
        row = lax.broadcasted_iota(jnp.int32, scores.shape, 0) + first
        scores = jnp.where(row >= lax.broadcasted_iota(jnp.int32, scores.shape, 1), scores, NEG)
        peak = jnp.max(scores, 1, keepdims=True)
        weights = jnp.exp2((scores - peak) * POWER)
        total = jnp.sum(weights, 1, keepdims=True)
        mixed = jnp.dot(weights.astype(BF16), kv[BLK:, HEAD:], preferred_element_type=F32)
        final = jnp.maximum(top, peak)
        w_ctx = jnp.exp2((top - final) * POWER)
        w_self = jnp.exp2((peak - final) * POWER)
        done = (mixed_all * w_ctx + mixed * w_self) / (total_all * w_ctx + total * w_self)
        result_at(c)[...] = done.astype(BF16)
        others(lambda n: result_to(n).start())

    def attend(head):
        bias = jnp.where(c > 0, 0.0, NEG).astype(F32)
        tile = BLK // 2
        for n in range(2):
            span = (n + 1) * tile
            q = q_s[head, n * tile : span, :]
            far = dot_nt(q, akv[:, :HEAD])
            near = dot_nt(q, kv[:span, :HEAD])
            row = lax.broadcasted_iota(jnp.int32, near.shape, 0) + n * tile
            near = jnp.where(row >= lax.broadcasted_iota(jnp.int32, near.shape, 1), near, NEG)
            peak = jnp.maximum(
                jnp.max(far, 1, keepdims=True) + bias, jnp.max(near, 1, keepdims=True)
            )
            far = jnp.exp2((far - (peak - bias)) * POWER)
            near = jnp.exp2((near - peak) * POWER)
            total = jnp.sum(far, 1, keepdims=True) + jnp.sum(near, 1, keepdims=True)
            mixed = jnp.dot(far.astype(BF16), akv[:, HEAD:], preferred_element_type=F32)
            mixed += jnp.dot(near.astype(BF16), kv[:span, HEAD:], preferred_element_type=F32)
            out_ref[n * tile : span, pl.ds(pl.multiple_of(head * HEAD, HEAD), HEAD)] = (
                mixed / total
            ).astype(BF16)

    def attend_pair(pair):
        @pl.loop(0, 2)
        def _(hh):
            attend(pair * 2 + hh)

    depth = jnp.where(y == 3, 1, y) + jnp.minimum(z, NZ - z)

    def anchor_copy(first, count, target, line, place):
        piece = akv.at[pl.ds(first, count)]
        return pltpu.make_async_remote_copy(
            src_ref=piece, dst_ref=piece, send_sem=a_send.at[line], recv_sem=a_recv.at[place],
            device_id=(target, t), device_id_type=MESH,
        )

    PIECE = BLK // 4
    HALF = BLK // 2

    def anchor_lines(act):
        @pl.when((z == 0) & (y < 2))
        def _():
            act(ctx_at(1, 0), 0)

        @pl.when(c == 0)
        def _():
            act(ctx_at(-1, 0), 1)

        @pl.when(z < 3)
        def _():
            act(ctx_at(0, 1), 2)

        @pl.when((z > 5) | (z == 0))
        def _():
            act(ctx_at(0, -1), 3)

    def anchor_piece(k, target, line):
        return anchor_copy(pl.multiple_of(k * PIECE, PIECE), PIECE, target, line, k)

    def anchor_step(g):
        k = g - depth

        @pl.when((k >= 0) & (k < 4))
        def _():
            @pl.when(depth > 0)
            def _():
                anchor_piece(k, ctx_at(0, 1), 2).wait_recv()

            anchor_lines(lambda target, line: anchor_piece(k, target, line).start())

            @pl.when((z == 3) & (k < 2))
            def _():
                anchor_piece(k, ctx_at(0, 1), 2).start()

            @pl.when((z == 5) & (k >= 2))
            def _():
                anchor_piece(k, ctx_at(0, -1), 3).start()

    def all_angles():
        for n in range(4):
            block_angles(n * (BLK // 4), BLK // 4)
        query_angles()

    def heads(pair):
        return lambda: attend_pair(pair)

    def queries(pair):
        return lambda: project_pair(pair)

    def anchor_root():
        @pl.when(c == 0)
        def _():
            akv[...] = kv[:BLK, :]

    def anchor_end():
        anchor_lines(lambda target, line: anchor_copy(0, BLK, target, line, 0).wait_send())

        @pl.when(z == 3)
        def _():
            anchor_copy(0, HALF, ctx_at(0, 1), 2, 0).wait_send()

        @pl.when(z == 5)
        def _():
            anchor_copy(0, HALF, ctx_at(0, -1), 3, 0).wait_send()

    TASKS = {
        0: (all_angles,),
        2: (x_second,),
        4: (x_third,),
        6: (x_fourth, x_last, project_kv, anchor_root,),
        7: (query_terms,),
        9: (queries(0),),
        10: (query_sum,),
        12: (heads(0), queries(1), query_part,),
        13: (heads(1),),
        15: (queries(2), query_merge,),
        16: (last_first,),
        17: (heads(2), last_second,),
    }

    x_first()

    @pl.loop(0, BLOCKS + LAG)
    def _(i):
        for r in range(STAGGER):
            calls = 0
            for s in reversed(range(7)):
                if s % STAGGER == r:
                    b = i - s // STAGGER

                    @pl.when((b >= 0) & (b < BLOCKS))
                    def _():
                        step(b, s)

                    if calls < 2:
                        anchor_step(2 * (STAGGER * i + r - ANCHOR_SLOT) + calls)
                        calls += 1

            for slot, acts in TASKS.items():
                if slot % STAGGER == r:

                    @pl.when(i == slot // STAGGER)
                    def _():
                        for act in acts:
                            act()

    last_third()
    attend_pair(3)
    of_all(4).wait_recv()

    for kind in range(5):
        of_all(kind).wait_send()

    @pl.loop(0, BLOCKS)
    def _(b):
        for line in range(4):
            rows = (3 * CUT // 2 + 8 * (3 * REST // 2)) if line < 2 else 7 * REST // 2 + 4 * (7 * CUT // 2)
            w_copy(b, pl.ds(0, rows), ctx_at(1, 0), line, 0).wait_send()

    for way in (0, 1):
        for chunk in range(4):
            x_near(way, chunk, 0).wait_send()
        for chunk in FAR[way]:
            x_far(way, chunk, 0).wait_send()
    for dx in (0, 1, -1, 2):
        x_across(dx).wait_send()
    anchor_end()


def on_device(rows, query_rows, positions, bound, wq, wk, wv):
    freq = np.asarray(rope_table(HEAD // 2) * 2, np.float32)[None]
    anywhere = pl.BlockSpec(memory_space=pl.ANY)
    vmem = pl.BlockSpec(memory_space=pltpu.VMEM)
    dma = pltpu.SemaphoreType.DMA
    return pl.pallas_call(
        kernel,
        out_shape=(
            pltpu.VMEM((BLK, 8 * HEAD), BF16),
            pltpu.VMEM((QT, 8 * HEAD), BF16),
        ),
        in_specs=[anywhere] * 5 + [vmem] * 3,
        out_specs=(vmem, vmem),
        scratch_shapes=[
            pltpu.VMEM((BLOCKS, N_CTX * SHARD, COLS), BF16),
            pltpu.VMEM((8, ROWS, FEATS), BF16),
            pltpu.VMEM((ROWS, HEAD), F32),
            pltpu.VMEM((ROWS, HEAD), F32),
            pltpu.VMEM((ROWS, COLS), F32),
            pltpu.VMEM((ROWS, COLS), BF16),
            pltpu.VMEM((BLK, COLS), BF16),
            pltpu.VMEM((8, BLK, HEAD), BF16),
            pltpu.VMEM((8 * QT, HEAD), BF16),
            pltpu.VMEM((8 * QT, HEAD), F32),
            pltpu.VMEM((N_CTX, OWN, HEAD), F32),
            pltpu.VMEM((N_CTX, OWN, HEAD), BF16),
            pltpu.VMEM((N_CTX, OWN, HEAD), BF16),
            pltpu.VMEM((N_CTX, 8, HEAD), F32),
            pltpu.VMEM((N_CTX, 8, HEAD), F32),
            dma((3 + BLOCKS,)),
            dma((BLOCKS, 4)),
            dma((BLOCKS, PLACES)),
            dma((3, 4)),
            dma((3, 4)),
            dma((4,)),
            dma((4,)),
            dma((4,)),
            dma((4,)),
            dma((5,)),
            dma((5,)),
        ],
        compiler_params=pltpu.CompilerParams(
            collective_id=0, has_side_effects=True, vmem_limit_bytes=56 << 20
        ),
        name="star_prefill",
    )(rows, query_rows, wq, wk, wv, positions[None], bound[None], freq)


def solution(mesh):
    placed = (
        P("ctx", "tp"),
        P(None, "tp"),
        P(),
        P(),
        P("ctx", "tp"),
        P("ctx", "tp"),
        P("ctx", "tp"),
    )
    return jax.shard_map(
        on_device,
        mesh=mesh,
        in_specs=placed,
        out_specs=(P("ctx", "tp"), P(None, "tp")),
        check_vma=False,
    )
```

```python
import math

import jax
import jax.numpy as jnp
import numpy as np
from jax import lax
from jax.experimental import pallas as pl
from jax.experimental.pallas import tpu as pltpu
from jax.sharding import PartitionSpec as P

MESH = pl.DeviceIdType.MESH
HEAD = 128
NX, NY, NZ = 4, 4, 8
N_CTX = NY * NZ
BLK = 512
QT = 64
ROWS = BLK + QT
SHARD = 256
CUT = 96
REST = SHARD - CUT
BLOCKS = 5
COLS = 256
CHUNK = ROWS // 4
FEATS = 1024
STAGGER = 3
LAG = 2
ANCHOR_SLOT = 7
NEG = -1e30
POWER = math.log2(math.e) / math.sqrt(HEAD)
OWN = BLK // N_CTX
F32, BF16 = jnp.float32, jnp.bfloat16


def rope_table(half):
    values = []
    for index in range(half):
        freq = 500000.0 ** (-2.0 * index / (2.0 * half))
        wavelen = 2.0 * math.pi / freq
        if wavelen > 8192.0:
            values.append(freq / 8.0)
        elif wavelen < 2048.0:
            values.append(freq)
        else:
            smooth = (8192.0 / wavelen - 1.0) / 3.0
            values.append((1.0 - smooth) * freq / 8.0 + smooth * freq)
    return values


def bz_at(dist):
    return dist - 1


def by_at(off, stage):
    return 4 + (off % NZ) * 2 + stage - 1


def ay_at(stage):
    return 20 + stage - 1


def az_at(off, dist):
    return 22 + (off % NY) * 4 + dist - 1


PLACES = 38
SIGN = (1, -1)


def column(row):
    n = row.shape[1]
    same = lax.broadcasted_iota(jnp.int32, (n, n), 0) == lax.broadcasted_iota(jnp.int32, (n, n), 1)
    return jnp.sum(jnp.where(same, jnp.broadcast_to(row, (n, n)), 0.0), axis=1, keepdims=True)


def dot_nt(a, b):
    return lax.dot_general(a, b, (((1,), (1,)), ((), ())), preferred_element_type=F32)


def kernel(
    x_ref, xq_ref, wq_ref, wk_ref, wv_ref, pos_ref, bound_ref, freq_ref,
    out_ref, qout_ref,
    w_all, x_all, cos_s, sin_s, acc, kv, akv, q_s, qq_s, terms, term_in, mixed_out, mixed_in, level_out, level_in,
    local_sem, w_send, w_recv, x_send, x_recv, sib_send, sib_recv, a_send, a_recv,
    ex_send, ex_recv,
):
    c = lax.axis_index("ctx")
    t = lax.axis_index("tp")
    y, z = lax.div(c, NZ), lax.rem(c, NZ)
    x, core = lax.div(t, 2), lax.rem(t, 2)

    def ctx_at(dy, dz):
        return lax.rem(y + dy + NY, NY) * NZ + lax.rem(z + dz + NZ, NZ)

    def tp_at(dx):
        return lax.rem(x + dx + NX, NX) * 2 + core

    sibling = x * 2 + 1 - core

    locals_ = [
        pltpu.make_async_copy(x_ref, x_all.at[t, pl.ds(0, BLK)], local_sem.at[0]),
        pltpu.make_async_copy(xq_ref, x_all.at[t, pl.ds(BLK, QT)], local_sem.at[1]),
    ]
    own = pl.ds(pl.multiple_of(c * SHARD, SHARD), SHARD)
    locals_.append(pltpu.make_async_copy(wk_ref, w_all.at[0, own, pl.ds(0, HEAD)], local_sem.at[2]))
    locals_.append(pltpu.make_async_copy(wv_ref, w_all.at[0, own, pl.ds(HEAD, HEAD)], local_sem.at[3]))
    for b in range(1, BLOCKS):
        locals_.append(
            pltpu.make_async_copy(
                wq_ref.at[:, pl.ds((b - 1) * COLS, COLS)], w_all.at[b, own], local_sem.at[3 + b]
            )
        )
    for copy in locals_:
        copy.start()

    barrier = pltpu.get_barrier_semaphore()

    @pl.loop(1, N_CTX)
    def _(d):
        pl.semaphore_signal(barrier, inc=1, device_id=(lax.rem(c + d, N_CTX), t), device_id_type=MESH)

    for other in (tp_at(1), tp_at(-1), sibling):
        pl.semaphore_signal(barrier, inc=1, device_id=(c, other), device_id_type=MESH)
    pl.semaphore_wait(barrier, N_CTX - 1 + 3)
    for copy in locals_:
        copy.wait()

    def rows_of(origin, first, count, dist, full, way):
        if dist == full:
            half = count // 2
            first, count = first + (half if way else 0), half
        return pl.ds(pl.multiple_of(origin * SHARD + first, 16), count)

    def w_copy(blk, rows, target, line, place):
        piece = w_all.at[blk, rows]
        return pltpu.make_async_remote_copy(
            src_ref=piece, dst_ref=piece, send_sem=w_send.at[blk, line], recv_sem=w_recv.at[blk, place],
            device_id=(target, t), device_id_type=MESH,
        )

    def bz(blk, way, dist):
        s = SIGN[way]
        rows = rows_of(ctx_at(0, -s * (dist - 1)), CUT, REST, dist, 4, way)
        w_copy(blk, rows, ctx_at(0, s), 2 + way, bz_at(dist)).start()

    def by(blk, off, way, stage):
        s = SIGN[way]
        rows = rows_of(ctx_at(-s * (stage - 1), off), CUT, REST, stage, 2, way)
        w_copy(blk, rows, ctx_at(s, 0), way, by_at(off, stage)).start()

    def ay(blk, way, stage):
        s = SIGN[way]
        rows = rows_of(ctx_at(-s * (stage - 1), 0), 0, CUT, stage, 2, way)
        w_copy(blk, rows, ctx_at(s, 0), way, ay_at(stage)).start()

    def az(blk, off, way, dist):
        s = SIGN[way]
        rows = rows_of(ctx_at(off, -s * (dist - 1)), 0, CUT, dist, 4, way)
        w_copy(blk, rows, ctx_at(0, s), 2 + way, az_at(off, dist)).start()

    def both(make, blk, *args):
        *front, last = args
        for way in (0, 1):
            make(blk, *front, way, last)

    def got(blk, place, count):
        w_copy(blk, pl.ds(0, count), ctx_at(1, 0), 0, place).wait_recv()

    def step(blk, s):
        if s == 0:
            both(bz, blk, 1)
            both(ay, blk, 1)
            both(az, blk, 0, 1)
            both(by, blk, 0, 1)
            return
        if s <= 4:
            got(blk, bz_at(s), 2 * REST if s < 4 else REST)
            if s < 4:
                both(bz, blk, s + 1)
                both(by, blk, -s, 1)
                both(by, blk, s, 1)
            else:
                both(by, blk, 4, 1)
        if s == 1:
            got(blk, ay_at(1), 2 * CUT)
            both(ay, blk, 2)
            both(az, blk, -1, 1)
            both(az, blk, 1, 1)
        if s == 2:
            got(blk, ay_at(2), CUT)
            both(az, blk, 2, 1)
        for off, since in ((0, 0), (1, 1), (-1, 1), (2, 2)):
            dist = s - since
            if 1 <= dist <= 4:
                got(blk, az_at(off, dist), 2 * CUT if dist < 4 else CUT)
                if dist < 4:
                    both(az, blk, off, dist + 1)
        for group in range(5):
            offs = (0,) if group == 0 else (4,) if group == 4 else (-group, group)
            stage = s - group
            if 1 <= stage <= 2:
                for off in offs:
                    got(blk, by_at(off, stage), 2 * REST if stage == 1 else REST)
                    if stage == 1:
                        both(by, blk, off, 2)

    def x_copy(dx, rows, target, send, recv):
        piece = x_all.at[tp_at(dx), rows]
        return pltpu.make_async_remote_copy(
            src_ref=piece, dst_ref=piece, send_sem=send, recv_sem=recv,
            device_id=(c, target), device_id_type=MESH,
        )

    def x_near(way, chunk, hop):
        return x_copy(-SIGN[way] * hop, pl.ds(chunk * CHUNK, CHUNK), tp_at(SIGN[way]), x_send.at[way, chunk], x_recv.at[way, chunk])

    def x_far(way, chunk, hop):
        return x_copy(-SIGN[way] * (1 + hop), pl.ds(chunk * CHUNK, CHUNK), tp_at(SIGN[way]), x_send.at[2, chunk], x_recv.at[2, chunk])

    FAR = ((0, 1), (2, 3))

    def x_across(dx):
        piece = x_all.at[tp_at(dx)]
        return pltpu.make_async_remote_copy(
            src_ref=piece, dst_ref=piece, send_sem=sib_send.at[dx % 4], recv_sem=sib_recv.at[dx % 4],
            device_id=(c, sibling), device_id_type=MESH,
        )

    def x_arrives(dx):
        piece = x_all.at[lax.rem(x + dx + NX, NX) * 2 + 1 - core]
        return pltpu.make_async_remote_copy(
            src_ref=piece, dst_ref=piece, send_sem=sib_send.at[dx % 4], recv_sem=sib_recv.at[dx % 4],
            device_id=(c, sibling), device_id_type=MESH,
        )

    def x_first():
        for way in (0, 1):
            for chunk in FAR[way] + FAR[1 - way]:
                x_near(way, chunk, 0).start()
        x_across(0).start()

    def x_second():
        for way in (0, 1):
            for chunk in FAR[way]:
                x_near(way, chunk, 1).wait_recv()
                x_far(way, chunk, 0).start()

    def x_third():
        for way in (0, 1):
            for chunk in FAR[1 - way]:
                x_near(way, chunk, 1).wait_recv()
            x_across(-SIGN[way]).start()

    def x_fourth():
        for way in (0, 1):
            for chunk in FAR[way]:
                x_far(way, chunk, 1).wait_recv()
        x_across(2).start()

    def x_last():
        for dx in (0, 1, -1, 2):
            x_arrives(dx).wait_recv()

    def angles(first, positions):
        angle = positions * freq_ref[...]
        lane = lax.broadcasted_iota(jnp.int32, angle.shape, 1)
        cosine, sine = jnp.cos(angle), jnp.sin(angle)
        rows = pl.ds(first, angle.shape[0])
        cos_s[rows, :] = cosine
        sin_s[rows, :] = jnp.where(lane < HEAD // 2, -sine, sine)

    def block_angles(first, count):
        place = lax.broadcasted_iota(jnp.int32, (count, HEAD), 0) + (c * BLK + first)
        angles(first, place.astype(F32))

    def query_angles():
        place = column(pos_ref[...].astype(F32))
        angles(BLK, jnp.broadcast_to(place, (QT, HEAD)))

    def add_slice(b, n, rows):
        acc[:rows] += jnp.dot(
            x_all[n, :rows],
            w_all[b, pl.ds(pl.multiple_of(n * FEATS, FEATS), FEATS), :],
            preferred_element_type=F32,
        )

    def project(b, rows):
        acc[...] = jnp.zeros_like(acc)

        @pl.loop(0, 8)
        def _(n):
            add_slice(b, n, rows)

    mine, facing = lax.div(z, 4), 1 - lax.div(z, 4)

    def last_slices(*places):
        for dy, half in places:
            add_slice(BLOCKS - 1, lax.rem(y + dy + NY, NY) * 2 + half, BLK)

    def last_first():
        acc[...] = jnp.zeros_like(acc)
        last_slices((0, mine), (0, facing), (1, mine), (-1, mine))

    def last_second():
        last_slices((1, facing), (-1, facing), (2, mine))

    def last_third():
        last_slices((2, facing))
        for hh in range(2):
            keep_block(6 + hh, hh * HEAD)

    def rotate(first, count, lane):
        u = acc[first : first + count, lane : lane + HEAD]
        turned = u * cos_s[first : first + count] + pltpu.roll(u, HEAD // 2, 1) * sin_s[first : first + count]
        return turned.astype(BF16)

    def project_kv():
        project(0, ROWS)
        kv[:, :HEAD] = rotate(0, ROWS, 0)
        kv[:, HEAD:] = acc[:, HEAD:].astype(BF16)

    def keep_block(head, lane):
        q_s[head] = rotate(0, BLK, lane)

    def project_pair(pair):
        project(pair + 1, ROWS if pair < 2 else BLK)
        for hh in range(2):
            head = pair * 2 + hh
            keep_block(head, hh * HEAD)
            if pair < 2:
                qq_s[head * QT : (head + 1) * QT, :] = rotate(BLK, QT, hh * HEAD)

    def others(act):
        @pl.loop(1, N_CTX)
        def _(d):
            act(lax.rem(c + d, N_CTX))

    def own_rows(n):
        return pl.ds(pl.multiple_of(n * OWN, OWN), OWN)

    def exchange(source, target, kind, peer):
        return pltpu.make_async_remote_copy(
            src_ref=source, dst_ref=target, send_sem=ex_send.at[kind], recv_sem=ex_recv.at[kind],
            device_id=(peer, t), device_id_type=MESH,
        )

    def early_rows():
        return own_rows(N_CTX // 2 + lax.div(c, 2))

    def term_to(n):
        return exchange(terms.at[own_rows(lax.div(n, 2))], term_in.at[c], 0, n)

    def qq_to(n):
        return exchange(qq_s.at[early_rows()], qq_s.at[early_rows()], 1, n)

    def mixed_to(n):
        return exchange(mixed_out.at[n], mixed_in.at[c], 2, n)

    def level_to(n):
        return exchange(level_out.at[n], level_in.at[c], 3, n)

    def result_to(n):
        return exchange(result_at(c), result_at(c), 4, n)

    def of_all(kind):
        most = pl.ds(0, N_CTX - 1)
        rows = pl.ds(0, (N_CTX - 1) * OWN)
        piece = (term_in.at[most], qq_s.at[rows], mixed_in.at[most], level_in.at[most], qq_s.at[rows])[kind]
        return exchange(piece, piece, kind, ctx_at(1, 0))

    def query_terms():
        share = x_all[lax.div(c, 4), BLK:, pl.ds(pl.multiple_of(lax.rem(c, 4) * SHARD, SHARD), SHARD)]
        for pair in (2, 3):
            term = jnp.dot(share, w_all[pair + 1, own, :], preferred_element_type=F32)
            first = (pair - 2) * 2 * QT
            terms[first : first + QT, :] = term[:, :HEAD]
            terms[first + QT : first + 2 * QT, :] = term[:, HEAD:]

        @pl.when(lax.rem(c, 2) == 0)
        def _():
            term_in[c] = terms[own_rows(lax.div(c, 2)), :]

        @pl.loop(0, N_CTX // 2)
        def _(d):
            n = 2 * lax.rem(lax.div(c, 2) + d, N_CTX // 2)

            @pl.when(n != c)
            def _():
                term_to(n).start()

    def query_sum():
        @pl.when(lax.rem(c, 2) == 0)
        def _():
            of_all(0).wait_recv()
            u = jnp.sum(term_in[...], 0)
            first = BLK + lax.rem(lax.div(c, 2), QT // OWN) * OWN
            place = pl.ds(pl.multiple_of(first, OWN), OWN)
            turned = u * cos_s[place, :] + pltpu.roll(u, HEAD // 2, 1) * sin_s[place, :]
            qq_s[early_rows(), :] = turned.astype(BF16)
            others(lambda n: qq_to(n).start())

    def by_parity(kind, even, odd, act):
        buffer = term_in if kind == 0 else qq_s
        for parity, count in ((0, even), (1, odd)):
            if count:

                @pl.when(lax.rem(c, 2) == parity)
                def _():
                    piece = buffer.at[pl.ds(0, count if kind == 0 else count * OWN)]
                    act(exchange(piece, piece, kind, ctx_at(1, 0)))

    def query_part():
        by_parity(1, N_CTX // 2 - 1, N_CTX // 2, lambda copy: copy.wait_recv())
        bound = column(bound_ref[...].astype(F32))
        bound = jnp.concatenate([bound] * 2, 0)

        @pl.loop(0, 4)
        def _(pair):
            rows = pl.ds(pl.multiple_of(pair * 2 * QT, 2 * QT), 2 * QT)
            scores = dot_nt(qq_s[rows, :], kv[:BLK, :HEAD])
            place = (lax.broadcasted_iota(jnp.int32, scores.shape, 1) + c * BLK).astype(F32)
            scores = jnp.where(place < bound, scores, NEG)
            peak = jnp.max(scores, 1, keepdims=True)
            weights = jnp.exp2((scores - peak) * POWER)
            total = jnp.sum(weights, 1, keepdims=True)
            mixed = jnp.dot(weights.astype(BF16), kv[:BLK, HEAD:], preferred_element_type=F32)
            for n in range(8):
                mixed_out[pair * 8 + n] = mixed[n * OWN : (n + 1) * OWN].astype(BF16)
            row = lax.broadcasted_iota(jnp.int32, mixed.shape, 0) & (OWN - 1)
            lane = lax.broadcasted_iota(jnp.int32, mixed.shape, 1)
            level = jnp.where(lane == row, peak, jnp.where(lane == row + OWN, total, 0.0))
            level = jnp.sum(level.reshape(8, OWN, HEAD), 1, keepdims=True)
            level_out[pl.ds(pl.multiple_of(pair * 8, 8), 8)] = level

        mixed_in[c] = mixed_out[c]
        level_in[c] = level_out[c]

        def both_to(n):
            mixed_to(n).start()
            level_to(n).start()

        others(both_to)

    def result_at(n):
        return qout_ref.at[
            pl.ds(pl.multiple_of(lax.rem(n, QT // OWN) * OWN, OWN), OWN),
            pl.ds(pl.multiple_of(lax.div(n, QT // OWN) * HEAD, HEAD), HEAD),
        ]

    def query_merge():
        of_all(2).wait_recv()
        of_all(3).wait_recv()

        def levels(first):
            shape = (N_CTX, OWN, HEAD)
            row = lax.broadcasted_iota(jnp.int32, shape, 1)
            lane = lax.broadcasted_iota(jnp.int32, shape, 2)
            kept = jnp.where(lane == row + first, jnp.broadcast_to(level_in[...], shape), 0.0)
            return jnp.sum(kept, 2, keepdims=True)

        peaks = levels(0)
        top = jnp.max(peaks, 0)
        scaled = jnp.exp2((peaks - top[None]) * POWER)
        total_all = jnp.sum(levels(OWN) * scaled, 0)
        mixed_all = jnp.sum(mixed_in[...].astype(F32) * scaled, 0)

        first = lax.rem(c, QT // OWN) * OWN
        scores = dot_nt(qq_s[own_rows(c), :], kv[BLK:, :HEAD])
        row = lax.broadcasted_iota(jnp.int32, scores.shape, 0) + first
        scores = jnp.where(row >= lax.broadcasted_iota(jnp.int32, scores.shape, 1), scores, NEG)
        peak = jnp.max(scores, 1, keepdims=True)
        weights = jnp.exp2((scores - peak) * POWER)
        total = jnp.sum(weights, 1, keepdims=True)
        mixed = jnp.dot(weights.astype(BF16), kv[BLK:, HEAD:], preferred_element_type=F32)
        final = jnp.maximum(top, peak)
        w_ctx = jnp.exp2((top - final) * POWER)
        w_self = jnp.exp2((peak - final) * POWER)
        done = (mixed_all * w_ctx + mixed * w_self) / (total_all * w_ctx + total * w_self)
        result_at(c)[...] = done.astype(BF16)
        others(lambda n: result_to(n).start())

    def attend(head):
        bias = jnp.where(c > 0, 0.0, NEG).astype(F32)
        tile = BLK // 2
        for n in range(2):
            span = (n + 1) * tile
            q = q_s[head, n * tile : span, :]
            far = dot_nt(q, akv[:, :HEAD])
            near = dot_nt(q, kv[:span, :HEAD])
            row = lax.broadcasted_iota(jnp.int32, near.shape, 0) + n * tile
            near = jnp.where(row >= lax.broadcasted_iota(jnp.int32, near.shape, 1), near, NEG)
            peak = jnp.maximum(
                jnp.max(far, 1, keepdims=True) + bias, jnp.max(near, 1, keepdims=True)
            )
            far = jnp.exp2((far - (peak - bias)) * POWER)
            near = jnp.exp2((near - peak) * POWER)
            total = jnp.sum(far, 1, keepdims=True) + jnp.sum(near, 1, keepdims=True)
            mixed = jnp.dot(far.astype(BF16), akv[:, HEAD:], preferred_element_type=F32)
            mixed += jnp.dot(near.astype(BF16), kv[:span, HEAD:], preferred_element_type=F32)
            out_ref[n * tile : span, pl.ds(pl.multiple_of(head * HEAD, HEAD), HEAD)] = (
                mixed / total
            ).astype(BF16)

    def attend_pair(pair):
        @pl.loop(0, 2)
        def _(hh):
            attend(pair * 2 + hh)

    depth = jnp.where(y == 3, 1, y) + jnp.minimum(z, NZ - z)

    def anchor_copy(first, count, target, line, place):
        piece = akv.at[pl.ds(first, count)]
        return pltpu.make_async_remote_copy(
            src_ref=piece, dst_ref=piece, send_sem=a_send.at[line], recv_sem=a_recv.at[place],
            device_id=(target, t), device_id_type=MESH,
        )

    PIECE = BLK // 4
    HALF = BLK // 2

    def anchor_lines(act):
        @pl.when((z == 0) & (y < 2))
        def _():
            act(ctx_at(1, 0), 0)

        @pl.when(c == 0)
        def _():
            act(ctx_at(-1, 0), 1)

        @pl.when(z < 3)
        def _():
            act(ctx_at(0, 1), 2)

        @pl.when((z > 5) | (z == 0))
        def _():
            act(ctx_at(0, -1), 3)

    def anchor_piece(k, target, line):
        return anchor_copy(pl.multiple_of(k * PIECE, PIECE), PIECE, target, line, k)

    def anchor_step(g):
        k = g - depth

        @pl.when((k >= 0) & (k < 4))
        def _():
            @pl.when(depth > 0)
            def _():
                anchor_piece(k, ctx_at(0, 1), 2).wait_recv()

            anchor_lines(lambda target, line: anchor_piece(k, target, line).start())

            @pl.when((z == 3) & (k < 2))
            def _():
                anchor_piece(k, ctx_at(0, 1), 2).start()

            @pl.when((z == 5) & (k >= 2))
            def _():
                anchor_piece(k, ctx_at(0, -1), 3).start()

    def all_angles():
        for n in range(4):
            block_angles(n * (BLK // 4), BLK // 4)
        query_angles()

    def heads(pair):
        return lambda: attend_pair(pair)

    def queries(pair):
        return lambda: project_pair(pair)

    def anchor_root():
        @pl.when(c == 0)
        def _():
            akv[...] = kv[:BLK, :]

    def anchor_end():
        anchor_lines(lambda target, line: anchor_copy(0, BLK, target, line, 0).wait_send())

        @pl.when(z == 3)
        def _():
            anchor_copy(0, HALF, ctx_at(0, 1), 2, 0).wait_send()

        @pl.when(z == 5)
        def _():
            anchor_copy(0, HALF, ctx_at(0, -1), 3, 0).wait_send()

    TASKS = {
        0: (all_angles,),
        2: (x_second,),
        4: (x_third,),
        6: (x_fourth, x_last, project_kv, anchor_root,),
        7: (query_terms,),
        9: (query_sum,),
        10: (queries(0),),
        11: (heads(0),),
        12: (queries(1),),
        13: (query_part,),
        14: (heads(1),),
        15: (query_merge, queries(2),),
        16: (last_first,),
        17: (heads(2), last_second,),
    }

    x_first()

    @pl.loop(0, BLOCKS + LAG)
    def _(i):
        for r in range(STAGGER):
            calls = 0
            for s in reversed(range(7)):
                if s % STAGGER == r:
                    b = i - s // STAGGER

                    @pl.when((b >= 0) & (b < BLOCKS))
                    def _():
                        step(b, s)

                    if calls < 2:
                        anchor_step(2 * (STAGGER * i + r - ANCHOR_SLOT) + calls)
                        calls += 1

            for slot, acts in TASKS.items():
                if slot % STAGGER == r:

                    @pl.when(i == slot // STAGGER)
                    def _():
                        for act in acts:
                            act()

    last_third()
    attend_pair(3)
    of_all(4).wait_recv()

    by_parity(0, N_CTX // 2 - 1, N_CTX // 2, lambda copy: copy.wait_send())
    by_parity(1, N_CTX - 1, 0, lambda copy: copy.wait_send())
    for kind in (2, 3, 4):
        of_all(kind).wait_send()

    @pl.loop(0, BLOCKS)
    def _(b):
        for line in range(4):
            rows = (3 * CUT // 2 + 8 * (3 * REST // 2)) if line < 2 else 7 * REST // 2 + 4 * (7 * CUT // 2)
            w_copy(b, pl.ds(0, rows), ctx_at(1, 0), line, 0).wait_send()

    for way in (0, 1):
        for chunk in range(4):
            x_near(way, chunk, 0).wait_send()
        for chunk in FAR[way]:
            x_far(way, chunk, 0).wait_send()
    for dx in (0, 1, -1, 2):
        x_across(dx).wait_send()
    anchor_end()


def on_device(rows, query_rows, positions, bound, wq, wk, wv):
    freq = np.asarray(rope_table(HEAD // 2) * 2, np.float32)[None]
    anywhere = pl.BlockSpec(memory_space=pl.ANY)
    vmem = pl.BlockSpec(memory_space=pltpu.VMEM)
    dma = pltpu.SemaphoreType.DMA
    return pl.pallas_call(
        kernel,
        out_shape=(
            pltpu.VMEM((BLK, 8 * HEAD), BF16),
            pltpu.VMEM((QT, 8 * HEAD), BF16),
        ),
        in_specs=[anywhere] * 5 + [vmem] * 3,
        out_specs=(vmem, vmem),
        scratch_shapes=[
            pltpu.VMEM((BLOCKS, N_CTX * SHARD, COLS), BF16),
            pltpu.VMEM((8, ROWS, FEATS), BF16),
            pltpu.VMEM((ROWS, HEAD), F32),
            pltpu.VMEM((ROWS, HEAD), F32),
            pltpu.VMEM((ROWS, COLS), F32),
            pltpu.VMEM((ROWS, COLS), BF16),
            pltpu.VMEM((BLK, COLS), BF16),
            pltpu.VMEM((8, BLK, HEAD), BF16),
            pltpu.VMEM((8 * QT, HEAD), BF16),
            pltpu.VMEM((4 * QT, HEAD), F32),
            pltpu.VMEM((N_CTX, OWN, HEAD), F32),
            pltpu.VMEM((N_CTX, OWN, HEAD), BF16),
            pltpu.VMEM((N_CTX, OWN, HEAD), BF16),
            pltpu.VMEM((N_CTX, 1, HEAD), F32),
            pltpu.VMEM((N_CTX, 1, HEAD), F32),
            dma((3 + BLOCKS,)),
            dma((BLOCKS, 4)),
            dma((BLOCKS, PLACES)),
            dma((3, 4)),
            dma((3, 4)),
            dma((4,)),
            dma((4,)),
            dma((4,)),
            dma((4,)),
            dma((5,)),
            dma((5,)),
        ],
        compiler_params=pltpu.CompilerParams(
            collective_id=0, has_side_effects=True, vmem_limit_bytes=56 << 20
        ),
        name="star_prefill",
    )(rows, query_rows, wq, wk, wv, positions[None], bound[None], freq)


def solution(mesh):
    placed = (
        P("ctx", "tp"),
        P(None, "tp"),
        P(),
        P(),
        P("ctx", "tp"),
        P("ctx", "tp"),
        P("ctx", "tp"),
    )
    return jax.shard_map(
        on_device,
        mesh=mesh,
        in_specs=placed,
        out_specs=(P("ctx", "tp"), P(None, "tp")),
        check_vma=False,
    )
```

```python
import math

import jax
import jax.numpy as jnp
import numpy as np
from jax import lax
from jax.experimental import pallas as pl
from jax.experimental.pallas import tpu as pltpu
from jax.sharding import PartitionSpec as P

MESH = pl.DeviceIdType.MESH
HEAD = 128
NX, NY, NZ = 4, 4, 8
N_CTX = NY * NZ
BLK = 512
QT = 64
ROWS = BLK + QT
SHARD = 256
CUT = 96
REST = SHARD - CUT
BLOCKS = 5
COLS = 256
CHUNK = ROWS // 4
FEATS = 1024
STAGGER = 3
LAG = 2
ANCHOR_SLOT = 7
NEG = -1e30
POWER = math.log2(math.e) / math.sqrt(HEAD)
OWN = BLK // N_CTX
F32, BF16 = jnp.float32, jnp.bfloat16


def rope_table(half):
    values = []
    for index in range(half):
        freq = 500000.0 ** (-2.0 * index / (2.0 * half))
        wavelen = 2.0 * math.pi / freq
        if wavelen > 8192.0:
            values.append(freq / 8.0)
        elif wavelen < 2048.0:
            values.append(freq)
        else:
            smooth = (8192.0 / wavelen - 1.0) / 3.0
            values.append((1.0 - smooth) * freq / 8.0 + smooth * freq)
    return values


def bz_at(dist):
    return dist - 1


def by_at(off, stage):
    return 4 + (off % NZ) * 2 + stage - 1


def ay_at(stage):
    return 20 + stage - 1


def az_at(off, dist):
    return 22 + (off % NY) * 4 + dist - 1


PLACES = 38
SIGN = (1, -1)


def column(row):
    n = row.shape[1]
    same = lax.broadcasted_iota(jnp.int32, (n, n), 0) == lax.broadcasted_iota(jnp.int32, (n, n), 1)
    return jnp.sum(jnp.where(same, jnp.broadcast_to(row, (n, n)), 0.0), axis=1, keepdims=True)


def dot_nt(a, b):
    return lax.dot_general(a, b, (((1,), (1,)), ((), ())), preferred_element_type=F32)


def kernel(
    x_ref, xq_ref, wq_ref, wk_ref, wv_ref, pos_ref, bound_ref, freq_ref,
    out_ref, qout_ref,
    w_all, x_all, cos_s, sin_s, acc, kv, akv, q_s, qq_s, terms, term_in, mixed_out, mixed_in, level_out, level_in,
    local_sem, w_send, w_recv, x_send, x_recv, sib_send, sib_recv, a_send, a_recv,
    ex_send, ex_recv,
):
    c = lax.axis_index("ctx")
    t = lax.axis_index("tp")
    y, z = lax.div(c, NZ), lax.rem(c, NZ)
    x, core = lax.div(t, 2), lax.rem(t, 2)

    def ctx_at(dy, dz):
        return lax.rem(y + dy + NY, NY) * NZ + lax.rem(z + dz + NZ, NZ)

    def tp_at(dx):
        return lax.rem(x + dx + NX, NX) * 2 + core

    sibling = x * 2 + 1 - core

    locals_ = [
        pltpu.make_async_copy(x_ref, x_all.at[t, pl.ds(0, BLK)], local_sem.at[0]),
        pltpu.make_async_copy(xq_ref, x_all.at[t, pl.ds(BLK, QT)], local_sem.at[1]),
    ]
    own = pl.ds(pl.multiple_of(c * SHARD, SHARD), SHARD)
    locals_.append(pltpu.make_async_copy(wk_ref, w_all.at[0, own, pl.ds(0, HEAD)], local_sem.at[2]))
    locals_.append(pltpu.make_async_copy(wv_ref, w_all.at[0, own, pl.ds(HEAD, HEAD)], local_sem.at[3]))
    for b in range(1, BLOCKS):
        locals_.append(
            pltpu.make_async_copy(
                wq_ref.at[:, pl.ds((b - 1) * COLS, COLS)], w_all.at[b, own], local_sem.at[3 + b]
            )
        )
    for copy in locals_:
        copy.start()

    barrier = pltpu.get_barrier_semaphore()

    @pl.loop(1, N_CTX)
    def _(d):
        pl.semaphore_signal(barrier, inc=1, device_id=(lax.rem(c + d, N_CTX), t), device_id_type=MESH)

    for other in (tp_at(1), tp_at(-1), sibling):
        pl.semaphore_signal(barrier, inc=1, device_id=(c, other), device_id_type=MESH)
    pl.semaphore_wait(barrier, N_CTX - 1 + 3)
    for copy in locals_:
        copy.wait()

    def rows_of(origin, first, count, dist, full, way):
        if dist == full:
            half = count // 2
            first, count = first + (half if way else 0), half
        return pl.ds(pl.multiple_of(origin * SHARD + first, 16), count)

    def w_copy(blk, rows, target, line, place):
        piece = w_all.at[blk, rows]
        return pltpu.make_async_remote_copy(
            src_ref=piece, dst_ref=piece, send_sem=w_send.at[blk, line], recv_sem=w_recv.at[blk, place],
            device_id=(target, t), device_id_type=MESH,
        )

    def bz(blk, way, dist):
        s = SIGN[way]
        rows = rows_of(ctx_at(0, -s * (dist - 1)), CUT, REST, dist, 4, way)
        w_copy(blk, rows, ctx_at(0, s), 2 + way, bz_at(dist)).start()

    def by(blk, off, way, stage):
        s = SIGN[way]
        rows = rows_of(ctx_at(-s * (stage - 1), off), CUT, REST, stage, 2, way)
        w_copy(blk, rows, ctx_at(s, 0), way, by_at(off, stage)).start()

    def ay(blk, way, stage):
        s = SIGN[way]
        rows = rows_of(ctx_at(-s * (stage - 1), 0), 0, CUT, stage, 2, way)
        w_copy(blk, rows, ctx_at(s, 0), way, ay_at(stage)).start()

    def az(blk, off, way, dist):
        s = SIGN[way]
        rows = rows_of(ctx_at(off, -s * (dist - 1)), 0, CUT, dist, 4, way)
        w_copy(blk, rows, ctx_at(0, s), 2 + way, az_at(off, dist)).start()

    def both(make, blk, *args):
        *front, last = args
        for way in (0, 1):
            make(blk, *front, way, last)

    def got(blk, place, count):
        w_copy(blk, pl.ds(0, count), ctx_at(1, 0), 0, place).wait_recv()

    def step(blk, s):
        if s == 0:
            both(bz, blk, 1)
            both(ay, blk, 1)
            both(az, blk, 0, 1)
            both(by, blk, 0, 1)
            return
        if s <= 4:
            got(blk, bz_at(s), 2 * REST if s < 4 else REST)
            if s < 4:
                both(bz, blk, s + 1)
                both(by, blk, -s, 1)
                both(by, blk, s, 1)
            else:
                both(by, blk, 4, 1)
        if s == 1:
            got(blk, ay_at(1), 2 * CUT)
            both(ay, blk, 2)
            both(az, blk, -1, 1)
            both(az, blk, 1, 1)
        if s == 2:
            got(blk, ay_at(2), CUT)
            both(az, blk, 2, 1)
        for off, since in ((0, 0), (1, 1), (-1, 1), (2, 2)):
            dist = s - since
            if 1 <= dist <= 4:
                got(blk, az_at(off, dist), 2 * CUT if dist < 4 else CUT)
                if dist < 4:
                    both(az, blk, off, dist + 1)
        for group in range(5):
            offs = (0,) if group == 0 else (4,) if group == 4 else (-group, group)
            stage = s - group
            if 1 <= stage <= 2:
                for off in offs:
                    got(blk, by_at(off, stage), 2 * REST if stage == 1 else REST)
                    if stage == 1:
                        both(by, blk, off, 2)

    def x_copy(dx, rows, target, send, recv):
        piece = x_all.at[tp_at(dx), rows]
        return pltpu.make_async_remote_copy(
            src_ref=piece, dst_ref=piece, send_sem=send, recv_sem=recv,
            device_id=(c, target), device_id_type=MESH,
        )

    def x_near(way, chunk, hop):
        return x_copy(-SIGN[way] * hop, pl.ds(chunk * CHUNK, CHUNK), tp_at(SIGN[way]), x_send.at[way, chunk], x_recv.at[way, chunk])

    def x_far(way, chunk, hop):
        return x_copy(-SIGN[way] * (1 + hop), pl.ds(chunk * CHUNK, CHUNK), tp_at(SIGN[way]), x_send.at[2, chunk], x_recv.at[2, chunk])

    FAR = ((0, 1), (2, 3))

    def x_across(dx):
        piece = x_all.at[tp_at(dx)]
        return pltpu.make_async_remote_copy(
            src_ref=piece, dst_ref=piece, send_sem=sib_send.at[dx % 4], recv_sem=sib_recv.at[dx % 4],
            device_id=(c, sibling), device_id_type=MESH,
        )

    def x_arrives(dx):
        piece = x_all.at[lax.rem(x + dx + NX, NX) * 2 + 1 - core]
        return pltpu.make_async_remote_copy(
            src_ref=piece, dst_ref=piece, send_sem=sib_send.at[dx % 4], recv_sem=sib_recv.at[dx % 4],
            device_id=(c, sibling), device_id_type=MESH,
        )

    def x_first():
        for way in (0, 1):
            for chunk in FAR[way] + FAR[1 - way]:
                x_near(way, chunk, 0).start()
        x_across(0).start()

    def x_second():
        for way in (0, 1):
            for chunk in FAR[way]:
                x_near(way, chunk, 1).wait_recv()
                x_far(way, chunk, 0).start()

    def x_third():
        for way in (0, 1):
            for chunk in FAR[1 - way]:
                x_near(way, chunk, 1).wait_recv()
            x_across(-SIGN[way]).start()

    def x_fourth():
        for way in (0, 1):
            for chunk in FAR[way]:
                x_far(way, chunk, 1).wait_recv()
        x_across(2).start()

    def x_last():
        for dx in (0, 1, -1, 2):
            x_arrives(dx).wait_recv()

    def angles(first, positions):
        angle = positions * freq_ref[...]
        lane = lax.broadcasted_iota(jnp.int32, angle.shape, 1)
        cosine, sine = jnp.cos(angle), jnp.sin(angle)
        rows = pl.ds(first, angle.shape[0])
        cos_s[rows, :] = cosine
        sin_s[rows, :] = jnp.where(lane < HEAD // 2, -sine, sine)

    def block_angles(first, count):
        place = lax.broadcasted_iota(jnp.int32, (count, HEAD), 0) + (c * BLK + first)
        angles(first, place.astype(F32))

    def query_angles():
        place = column(pos_ref[...].astype(F32))
        angles(BLK, jnp.broadcast_to(place, (QT, HEAD)))

    def add_slice(b, n, rows):
        acc[:rows] += jnp.dot(
            x_all[n, :rows],
            w_all[b, pl.ds(pl.multiple_of(n * FEATS, FEATS), FEATS), :],
            preferred_element_type=F32,
        )

    def project(b, rows):
        acc[...] = jnp.zeros_like(acc)

        @pl.loop(0, 8)
        def _(n):
            add_slice(b, n, rows)

    mine, facing = lax.div(z, 4), 1 - lax.div(z, 4)

    def last_slices(*places):
        for dy, half in places:
            add_slice(BLOCKS - 1, lax.rem(y + dy + NY, NY) * 2 + half, BLK)

    def last_first():
        acc[...] = jnp.zeros_like(acc)
        last_slices((0, mine), (0, facing), (1, mine), (-1, mine))

    def last_second():
        last_slices((1, facing), (-1, facing), (2, mine))

    def last_third():
        last_slices((2, facing))
        for hh in range(2):
            keep_block(6 + hh, hh * HEAD)

    def rotate(first, count, lane):
        u = acc[first : first + count, lane : lane + HEAD]
        turned = u * cos_s[first : first + count] + pltpu.roll(u, HEAD // 2, 1) * sin_s[first : first + count]
        return turned.astype(BF16)

    def project_kv():
        project(0, ROWS)
        kv[:, :HEAD] = rotate(0, ROWS, 0)
        kv[:, HEAD:] = acc[:, HEAD:].astype(BF16)

    def keep_block(head, lane):
        q_s[head] = rotate(0, BLK, lane)

    def project_pair(pair):
        project(pair + 1, ROWS if pair < 2 else BLK)
        for hh in range(2):
            head = pair * 2 + hh
            keep_block(head, hh * HEAD)
            if pair < 2:
                qq_s[head * QT : (head + 1) * QT, :] = rotate(BLK, QT, hh * HEAD)

    def others(act):
        @pl.loop(1, N_CTX)
        def _(d):
            act(lax.rem(c + d, N_CTX))

    def own_rows(n):
        return pl.ds(pl.multiple_of(n * OWN, OWN), OWN)

    def exchange(source, target, kind, peer):
        return pltpu.make_async_remote_copy(
            src_ref=source, dst_ref=target, send_sem=ex_send.at[kind], recv_sem=ex_recv.at[kind],
            device_id=(peer, t), device_id_type=MESH,
        )

    def early_rows():
        return own_rows(N_CTX // 2 + lax.div(c, 2))

    def term_to(n):
        return exchange(terms.at[own_rows(lax.div(n, 2))], term_in.at[c], 0, n)

    def qq_to(n):
        return exchange(qq_s.at[early_rows()], qq_s.at[early_rows()], 1, n)

    def mixed_to(n):
        return exchange(mixed_out.at[n], mixed_in.at[c], 2, n)

    def level_to(n):
        return exchange(level_out.at[n], level_in.at[c], 3, n)

    def result_to(n):
        return exchange(result_at(c), result_at(c), 4, n)

    def of_all(kind):
        most = pl.ds(0, N_CTX - 1)
        rows = pl.ds(0, (N_CTX - 1) * OWN)
        piece = (term_in.at[most], qq_s.at[rows], mixed_in.at[most], level_in.at[most], qq_s.at[rows])[kind]
        return exchange(piece, piece, kind, ctx_at(1, 0))

    def query_terms():
        share = x_all[lax.div(c, 4), BLK:, pl.ds(pl.multiple_of(lax.rem(c, 4) * SHARD, SHARD), SHARD)]
        for pair in (2, 3):
            term = jnp.dot(share, w_all[pair + 1, own, :], preferred_element_type=F32)
            first = (pair - 2) * 2 * QT
            terms[first : first + QT, :] = term[:, :HEAD]
            terms[first + QT : first + 2 * QT, :] = term[:, HEAD:]

        @pl.when(lax.rem(c, 2) == 0)
        def _():
            term_in[c] = terms[own_rows(lax.div(c, 2)), :]

        @pl.loop(0, N_CTX // 2)
        def _(d):
            n = 2 * lax.rem(lax.div(c, 2) + d, N_CTX // 2)

            @pl.when(n != c)
            def _():
                term_to(n).start()

    def query_sum():
        @pl.when(lax.rem(c, 2) == 0)
        def _():
            of_all(0).wait_recv()
            u = jnp.sum(term_in[...], 0)
            first = BLK + lax.rem(lax.div(c, 2), QT // OWN) * OWN
            place = pl.ds(pl.multiple_of(first, OWN), OWN)
            turned = u * cos_s[place, :] + pltpu.roll(u, HEAD // 2, 1) * sin_s[place, :]
            qq_s[early_rows(), :] = turned.astype(BF16)
            others(lambda n: qq_to(n).start())

    def by_parity(kind, even, odd, act):
        buffer = term_in if kind == 0 else qq_s
        for parity, count in ((0, even), (1, odd)):
            if count:

                @pl.when(lax.rem(c, 2) == parity)
                def _():
                    piece = buffer.at[pl.ds(0, count if kind == 0 else count * OWN)]
                    act(exchange(piece, piece, kind, ctx_at(1, 0)))

    def query_part():
        by_parity(1, N_CTX // 2 - 1, N_CTX // 2, lambda copy: copy.wait_recv())
        bound = column(bound_ref[...].astype(F32))
        bound = jnp.concatenate([bound] * 2, 0)

        @pl.loop(0, 4)
        def _(pair):
            rows = pl.ds(pl.multiple_of(pair * 2 * QT, 2 * QT), 2 * QT)
            scores = dot_nt(qq_s[rows, :], kv[:BLK, :HEAD])
            place = (lax.broadcasted_iota(jnp.int32, scores.shape, 1) + c * BLK).astype(F32)
            scores = jnp.where(place < bound, scores, NEG)
            peak = jnp.max(scores, 1, keepdims=True)
            weights = jnp.exp2((scores - peak) * POWER)
            total = jnp.sum(weights, 1, keepdims=True)
            mixed = jnp.dot(weights.astype(BF16), kv[:BLK, HEAD:], preferred_element_type=F32)
            for n in range(8):
                mixed_out[pair * 8 + n] = mixed[n * OWN : (n + 1) * OWN].astype(BF16)
            row = lax.broadcasted_iota(jnp.int32, mixed.shape, 0) & (OWN - 1)
            lane = lax.broadcasted_iota(jnp.int32, mixed.shape, 1)
            level = jnp.where(lane == row, peak, jnp.where(lane == row + OWN, total, 0.0))
            level = jnp.sum(level.reshape(8, OWN, HEAD), 1, keepdims=True)
            level_out[pl.ds(pl.multiple_of(pair * 8, 8), 8)] = level

        mixed_in[c] = mixed_out[c]
        level_in[c] = level_out[c]

        def both_to(n):
            mixed_to(n).start()
            level_to(n).start()

        others(both_to)

    def result_at(n):
        return qout_ref.at[
            pl.ds(pl.multiple_of(lax.rem(n, QT // OWN) * OWN, OWN), OWN),
            pl.ds(pl.multiple_of(lax.div(n, QT // OWN) * HEAD, HEAD), HEAD),
        ]

    def query_merge():
        of_all(2).wait_recv()
        of_all(3).wait_recv()

        def levels(first):
            shape = (N_CTX, OWN, HEAD)
            row = lax.broadcasted_iota(jnp.int32, shape, 1)
            lane = lax.broadcasted_iota(jnp.int32, shape, 2)
            kept = jnp.where(lane == row + first, jnp.broadcast_to(level_in[...], shape), 0.0)
            return jnp.sum(kept, 2, keepdims=True)

        peaks = levels(0)
        top = jnp.max(peaks, 0)
        scaled = jnp.exp2((peaks - top[None]) * POWER)
        total_all = jnp.sum(levels(OWN) * scaled, 0)
        mixed_all = jnp.sum(mixed_in[...].astype(F32) * scaled, 0)

        first = lax.rem(c, QT // OWN) * OWN
        scores = dot_nt(qq_s[own_rows(c), :], kv[BLK:, :HEAD])
        row = lax.broadcasted_iota(jnp.int32, scores.shape, 0) + first
        scores = jnp.where(row >= lax.broadcasted_iota(jnp.int32, scores.shape, 1), scores, NEG)
        peak = jnp.max(scores, 1, keepdims=True)
        weights = jnp.exp2((scores - peak) * POWER)
        total = jnp.sum(weights, 1, keepdims=True)
        mixed = jnp.dot(weights.astype(BF16), kv[BLK:, HEAD:], preferred_element_type=F32)
        final = jnp.maximum(top, peak)
        w_ctx = jnp.exp2((top - final) * POWER)
        w_self = jnp.exp2((peak - final) * POWER)
        done = (mixed_all * w_ctx + mixed * w_self) / (total_all * w_ctx + total * w_self)
        result_at(c)[...] = done.astype(BF16)
        others(lambda n: result_to(n).start())

    def attend(head):
        bias = jnp.where(c > 0, 0.0, NEG).astype(F32)
        tile = BLK // 2
        for n in range(2):
            span = (n + 1) * tile
            q = q_s[head, n * tile : span, :]
            far = dot_nt(q, akv[:, :HEAD])
            near = dot_nt(q, kv[:span, :HEAD])
            row = lax.broadcasted_iota(jnp.int32, near.shape, 0) + n * tile
            near = jnp.where(row >= lax.broadcasted_iota(jnp.int32, near.shape, 1), near, NEG)
            peak = jnp.maximum(
                jnp.max(far, 1, keepdims=True) + bias, jnp.max(near, 1, keepdims=True)
            )
            far = jnp.exp2((far - (peak - bias)) * POWER)
            near = jnp.exp2((near - peak) * POWER)
            total = jnp.sum(far, 1, keepdims=True) + jnp.sum(near, 1, keepdims=True)
            mixed = jnp.dot(far.astype(BF16), akv[:, HEAD:], preferred_element_type=F32)
            mixed += jnp.dot(near.astype(BF16), kv[:span, HEAD:], preferred_element_type=F32)
            out_ref[n * tile : span, pl.ds(pl.multiple_of(head * HEAD, HEAD), HEAD)] = (
                mixed / total
            ).astype(BF16)

    def attend_pair(pair):
        @pl.loop(0, 2)
        def _(hh):
            attend(pair * 2 + hh)

    depth = jnp.where(y == 3, 1, y) + jnp.minimum(z, NZ - z)

    def anchor_copy(first, count, target, line, place):
        piece = akv.at[pl.ds(first, count)]
        return pltpu.make_async_remote_copy(
            src_ref=piece, dst_ref=piece, send_sem=a_send.at[line], recv_sem=a_recv.at[place],
            device_id=(target, t), device_id_type=MESH,
        )

    PIECE = BLK // 2
    HALF = BLK // 2

    def anchor_lines(act):
        @pl.when((z == 0) & (y < 2))
        def _():
            act(ctx_at(1, 0), 0)

        @pl.when(c == 0)
        def _():
            act(ctx_at(-1, 0), 1)

        @pl.when(z < 3)
        def _():
            act(ctx_at(0, 1), 2)

        @pl.when((z > 5) | (z == 0))
        def _():
            act(ctx_at(0, -1), 3)

    def anchor_piece(k, target, line):
        return anchor_copy(pl.multiple_of(k * PIECE, PIECE), PIECE, target, line, k)

    def anchor_step(g):
        k = g - depth

        @pl.when((k >= 0) & (k < 2))
        def _():
            @pl.when(depth > 0)
            def _():
                anchor_piece(k, ctx_at(0, 1), 2).wait_recv()

            anchor_lines(lambda target, line: anchor_piece(k, target, line).start())

            @pl.when((z == 3) & (k < 1))
            def _():
                anchor_piece(k, ctx_at(0, 1), 2).start()

            @pl.when((z == 5) & (k >= 1))
            def _():
                anchor_piece(k, ctx_at(0, -1), 3).start()

    def all_angles():
        for n in range(4):
            block_angles(n * (BLK // 4), BLK // 4)
        query_angles()

    def heads(pair):
        return lambda: attend_pair(pair)

    def queries(pair):
        return lambda: project_pair(pair)

    def anchor_root():
        @pl.when(c == 0)
        def _():
            akv[...] = kv[:BLK, :]

    def anchor_end():
        anchor_lines(lambda target, line: anchor_copy(0, BLK, target, line, 0).wait_send())

        @pl.when(z == 3)
        def _():
            anchor_copy(0, HALF, ctx_at(0, 1), 2, 0).wait_send()

        @pl.when(z == 5)
        def _():
            anchor_copy(0, HALF, ctx_at(0, -1), 3, 0).wait_send()

    TASKS = {
        0: (all_angles,),
        2: (x_second,),
        4: (x_third,),
        6: (x_fourth, x_last, project_kv, anchor_root,),
        7: (query_terms,),
        9: (query_sum,),
        10: (queries(0),),
        12: (queries(1),),
        13: (query_part,),
        14: (heads(0),),
        15: (query_merge, queries(2),),
        16: (last_first, heads(1),),
        17: (heads(2), last_second,),
    }

    x_first()

    @pl.loop(0, BLOCKS + LAG)
    def _(i):
        for r in range(STAGGER):
            for s in reversed(range(7)):
                if s % STAGGER == r:
                    b = i - s // STAGGER

                    @pl.when((b >= 0) & (b < BLOCKS))
                    def _():
                        step(b, s)

            anchor_step(STAGGER * i + r - ANCHOR_SLOT)

            for slot, acts in TASKS.items():
                if slot % STAGGER == r:

                    @pl.when(i == slot // STAGGER)
                    def _():
                        for act in acts:
                            act()

    last_third()
    attend_pair(3)
    of_all(4).wait_recv()

    by_parity(0, N_CTX // 2 - 1, N_CTX // 2, lambda copy: copy.wait_send())
    by_parity(1, N_CTX - 1, 0, lambda copy: copy.wait_send())
    for kind in (2, 3, 4):
        of_all(kind).wait_send()

    @pl.loop(0, BLOCKS)
    def _(b):
        for line in range(4):
            rows = (3 * CUT // 2 + 8 * (3 * REST // 2)) if line < 2 else 7 * REST // 2 + 4 * (7 * CUT // 2)
            w_copy(b, pl.ds(0, rows), ctx_at(1, 0), line, 0).wait_send()

    for way in (0, 1):
        for chunk in range(4):
            x_near(way, chunk, 0).wait_send()
        for chunk in FAR[way]:
            x_far(way, chunk, 0).wait_send()
    for dx in (0, 1, -1, 2):
        x_across(dx).wait_send()
    anchor_end()


def on_device(rows, query_rows, positions, bound, wq, wk, wv):
    freq = np.asarray(rope_table(HEAD // 2) * 2, np.float32)[None]
    anywhere = pl.BlockSpec(memory_space=pl.ANY)
    vmem = pl.BlockSpec(memory_space=pltpu.VMEM)
    dma = pltpu.SemaphoreType.DMA
    return pl.pallas_call(
        kernel,
        out_shape=(
            pltpu.VMEM((BLK, 8 * HEAD), BF16),
            pltpu.VMEM((QT, 8 * HEAD), BF16),
        ),
        in_specs=[anywhere] * 5 + [vmem] * 3,
        out_specs=(vmem, vmem),
        scratch_shapes=[
            pltpu.VMEM((BLOCKS, N_CTX * SHARD, COLS), BF16),
            pltpu.VMEM((8, ROWS, FEATS), BF16),
            pltpu.VMEM((ROWS, HEAD), F32),
            pltpu.VMEM((ROWS, HEAD), F32),
            pltpu.VMEM((ROWS, COLS), F32),
            pltpu.VMEM((ROWS, COLS), BF16),
            pltpu.VMEM((BLK, COLS), BF16),
            pltpu.VMEM((8, BLK, HEAD), BF16),
            pltpu.VMEM((8 * QT, HEAD), BF16),
            pltpu.VMEM((4 * QT, HEAD), F32),
            pltpu.VMEM((N_CTX, OWN, HEAD), F32),
            pltpu.VMEM((N_CTX, OWN, HEAD), BF16),
            pltpu.VMEM((N_CTX, OWN, HEAD), BF16),
            pltpu.VMEM((N_CTX, 1, HEAD), F32),
            pltpu.VMEM((N_CTX, 1, HEAD), F32),
            dma((3 + BLOCKS,)),
            dma((BLOCKS, 4)),
            dma((BLOCKS, PLACES)),
            dma((3, 4)),
            dma((3, 4)),
            dma((4,)),
            dma((4,)),
            dma((4,)),
            dma((4,)),
            dma((5,)),
            dma((5,)),
        ],
        compiler_params=pltpu.CompilerParams(
            collective_id=0, has_side_effects=True, vmem_limit_bytes=56 << 20
        ),
        name="star_prefill",
    )(rows, query_rows, wq, wk, wv, positions[None], bound[None], freq)


def solution(mesh):
    placed = (
        P("ctx", "tp"),
        P(None, "tp"),
        P(),
        P(),
        P("ctx", "tp"),
        P("ctx", "tp"),
        P("ctx", "tp"),
    )
    return jax.shard_map(
        on_device,
        mesh=mesh,
        in_specs=placed,
        out_specs=(P("ctx", "tp"), P(None, "tp")),
        check_vma=False,
    )
```

```python
import math

import jax
import jax.numpy as jnp
import numpy as np
from jax import lax
from jax.experimental import pallas as pl
from jax.experimental.pallas import tpu as pltpu
from jax.sharding import PartitionSpec as P

MESH = pl.DeviceIdType.MESH
HEAD = 128
NX, NY, NZ = 4, 4, 8
N_CTX = NY * NZ
BLK = 512
QT = 64
ROWS = BLK + QT
SHARD = 256
CUT = 96
REST = SHARD - CUT
BLOCKS = 5
COLS = 256
CHUNK = ROWS // 4
FEATS = 1024
STAGGER = 3
LAG = 2
ANCHOR_SLOT = 7
NEG = -1e30
POWER = math.log2(math.e) / math.sqrt(HEAD)
OWN = BLK // N_CTX
F32, BF16 = jnp.float32, jnp.bfloat16


def rope_table(half):
    values = []
    for index in range(half):
        freq = 500000.0 ** (-2.0 * index / (2.0 * half))
        wavelen = 2.0 * math.pi / freq
        if wavelen > 8192.0:
            values.append(freq / 8.0)
        elif wavelen < 2048.0:
            values.append(freq)
        else:
            smooth = (8192.0 / wavelen - 1.0) / 3.0
            values.append((1.0 - smooth) * freq / 8.0 + smooth * freq)
    return values


def bz_at(dist):
    return dist - 1


def by_at(off, stage):
    return 4 + (off % NZ) * 2 + stage - 1


def ay_at(stage):
    return 20 + stage - 1


def az_at(off, dist):
    return 22 + (off % NY) * 4 + dist - 1


PLACES = 38
SIGN = (1, -1)


def column(row):
    n = row.shape[1]
    same = lax.broadcasted_iota(jnp.int32, (n, n), 0) == lax.broadcasted_iota(jnp.int32, (n, n), 1)
    return jnp.sum(jnp.where(same, jnp.broadcast_to(row, (n, n)), 0.0), axis=1, keepdims=True)


def dot_nt(a, b):
    return lax.dot_general(a, b, (((1,), (1,)), ((), ())), preferred_element_type=F32)


def kernel(
    x_ref, xq_ref, wq_ref, wk_ref, wv_ref, pos_ref, bound_ref, freq_ref,
    out_ref, qout_ref,
    w_all, x_all, cos_s, sin_s, acc, kv, akv, q_s, qq_s, terms, term_in, mixed_out, mixed_in, level_out, level_in,
    local_sem, w_send, w_recv, x_send, x_recv, sib_send, sib_recv, a_send, a_recv,
    ex_send, ex_recv,
):
    c = lax.axis_index("ctx")
    t = lax.axis_index("tp")
    y, z = lax.div(c, NZ), lax.rem(c, NZ)
    x, core = lax.div(t, 2), lax.rem(t, 2)

    def ctx_at(dy, dz):
        return lax.rem(y + dy + NY, NY) * NZ + lax.rem(z + dz + NZ, NZ)

    def tp_at(dx):
        return lax.rem(x + dx + NX, NX) * 2 + core

    sibling = x * 2 + 1 - core

    locals_ = [
        pltpu.make_async_copy(x_ref, x_all.at[t, pl.ds(0, BLK)], local_sem.at[0]),
        pltpu.make_async_copy(xq_ref, x_all.at[t, pl.ds(BLK, QT)], local_sem.at[1]),
    ]
    own = pl.ds(pl.multiple_of(c * SHARD, SHARD), SHARD)
    locals_.append(pltpu.make_async_copy(wk_ref, w_all.at[0, own, pl.ds(0, HEAD)], local_sem.at[2]))
    locals_.append(pltpu.make_async_copy(wv_ref, w_all.at[0, own, pl.ds(HEAD, HEAD)], local_sem.at[3]))
    for b in range(1, BLOCKS):
        locals_.append(
            pltpu.make_async_copy(
                wq_ref.at[:, pl.ds((b - 1) * COLS, COLS)], w_all.at[b, own], local_sem.at[3 + b]
            )
        )
    for copy in locals_:
        copy.start()

    barrier = pltpu.get_barrier_semaphore()

    for near in (ctx_at(1, 0), ctx_at(-1, 0), ctx_at(0, 1), ctx_at(0, -1)):
        pl.semaphore_signal(barrier, inc=1, device_id=(near, t), device_id_type=MESH)
    for other in (tp_at(1), tp_at(-1), sibling):
        pl.semaphore_signal(barrier, inc=1, device_id=(c, other), device_id_type=MESH)
    pl.semaphore_wait(barrier, 7)
    for copy in locals_:
        copy.wait()

    def rows_of(origin, first, count, dist, full, way):
        if dist == full:
            half = count // 2
            first, count = first + (half if way else 0), half
        return pl.ds(pl.multiple_of(origin * SHARD + first, 16), count)

    def w_copy(blk, rows, target, line, place):
        piece = w_all.at[blk, rows]
        return pltpu.make_async_remote_copy(
            src_ref=piece, dst_ref=piece, send_sem=w_send.at[blk, line], recv_sem=w_recv.at[blk, place],
            device_id=(target, t), device_id_type=MESH,
        )

    def bz(blk, way, dist):
        s = SIGN[way]
        rows = rows_of(ctx_at(0, -s * (dist - 1)), CUT, REST, dist, 4, way)
        w_copy(blk, rows, ctx_at(0, s), 2 + way, bz_at(dist)).start()

    def by(blk, off, way, stage):
        s = SIGN[way]
        rows = rows_of(ctx_at(-s * (stage - 1), off), CUT, REST, stage, 2, way)
        w_copy(blk, rows, ctx_at(s, 0), way, by_at(off, stage)).start()

    def ay(blk, way, stage):
        s = SIGN[way]
        rows = rows_of(ctx_at(-s * (stage - 1), 0), 0, CUT, stage, 2, way)
        w_copy(blk, rows, ctx_at(s, 0), way, ay_at(stage)).start()

    def az(blk, off, way, dist):
        s = SIGN[way]
        rows = rows_of(ctx_at(off, -s * (dist - 1)), 0, CUT, dist, 4, way)
        w_copy(blk, rows, ctx_at(0, s), 2 + way, az_at(off, dist)).start()

    def both(make, blk, *args):
        *front, last = args
        for way in (0, 1):
            make(blk, *front, way, last)

    def got(blk, place, count):
        w_copy(blk, pl.ds(0, count), ctx_at(1, 0), 0, place).wait_recv()

    def step(blk, s):
        if s == 0:
            both(bz, blk, 1)
            both(ay, blk, 1)
            both(az, blk, 0, 1)
            both(by, blk, 0, 1)
            return
        if s <= 4:
            got(blk, bz_at(s), 2 * REST if s < 4 else REST)
            if s < 4:
                both(bz, blk, s + 1)
                both(by, blk, -s, 1)
                both(by, blk, s, 1)
            else:
                both(by, blk, 4, 1)
        if s == 1:
            got(blk, ay_at(1), 2 * CUT)
            both(ay, blk, 2)
            both(az, blk, -1, 1)
            both(az, blk, 1, 1)
        if s == 2:
            got(blk, ay_at(2), CUT)
            both(az, blk, 2, 1)
        for off, since in ((0, 0), (1, 1), (-1, 1), (2, 2)):
            dist = s - since
            if 1 <= dist <= 4:
                got(blk, az_at(off, dist), 2 * CUT if dist < 4 else CUT)
                if dist < 4:
                    both(az, blk, off, dist + 1)
        for group in range(5):
            offs = (0,) if group == 0 else (4,) if group == 4 else (-group, group)
            stage = s - group
            if 1 <= stage <= 2:
                for off in offs:
                    got(blk, by_at(off, stage), 2 * REST if stage == 1 else REST)
                    if stage == 1:
                        both(by, blk, off, 2)

    def x_copy(dx, rows, target, send, recv):
        piece = x_all.at[tp_at(dx), rows]
        return pltpu.make_async_remote_copy(
            src_ref=piece, dst_ref=piece, send_sem=send, recv_sem=recv,
            device_id=(c, target), device_id_type=MESH,
        )

    def x_near(way, chunk, hop):
        return x_copy(-SIGN[way] * hop, pl.ds(chunk * CHUNK, CHUNK), tp_at(SIGN[way]), x_send.at[way, chunk], x_recv.at[way, chunk])

    def x_far(way, chunk, hop):
        return x_copy(-SIGN[way] * (1 + hop), pl.ds(chunk * CHUNK, CHUNK), tp_at(SIGN[way]), x_send.at[2, chunk], x_recv.at[2, chunk])

    FAR = ((0, 1), (2, 3))

    def x_across(dx):
        piece = x_all.at[tp_at(dx)]
        return pltpu.make_async_remote_copy(
            src_ref=piece, dst_ref=piece, send_sem=sib_send.at[dx % 4], recv_sem=sib_recv.at[dx % 4],
            device_id=(c, sibling), device_id_type=MESH,
        )

    def x_arrives(dx):
        piece = x_all.at[lax.rem(x + dx + NX, NX) * 2 + 1 - core]
        return pltpu.make_async_remote_copy(
            src_ref=piece, dst_ref=piece, send_sem=sib_send.at[dx % 4], recv_sem=sib_recv.at[dx % 4],
            device_id=(c, sibling), device_id_type=MESH,
        )

    def x_first():
        for way in (0, 1):
            for chunk in FAR[way] + FAR[1 - way]:
                x_near(way, chunk, 0).start()
        x_across(0).start()

    def x_second():
        for way in (0, 1):
            for chunk in FAR[way]:
                x_near(way, chunk, 1).wait_recv()
                x_far(way, chunk, 0).start()

    def x_third():
        for way in (0, 1):
            for chunk in FAR[1 - way]:
                x_near(way, chunk, 1).wait_recv()
            x_across(-SIGN[way]).start()

    def x_fourth():
        for way in (0, 1):
            for chunk in FAR[way]:
                x_far(way, chunk, 1).wait_recv()
        x_across(2).start()

    def x_last():
        for dx in (0, 1, -1, 2):
            x_arrives(dx).wait_recv()

    def angles(first, positions):
        angle = positions * freq_ref[...]
        lane = lax.broadcasted_iota(jnp.int32, angle.shape, 1)
        cosine, sine = jnp.cos(angle), jnp.sin(angle)
        rows = pl.ds(first, angle.shape[0])
        cos_s[rows, :] = cosine
        sin_s[rows, :] = jnp.where(lane < HEAD // 2, -sine, sine)

    def block_angles(first, count):
        place = lax.broadcasted_iota(jnp.int32, (count, HEAD), 0) + (c * BLK + first)
        angles(first, place.astype(F32))

    def query_angles():
        place = column(pos_ref[...].astype(F32))
        angles(BLK, jnp.broadcast_to(place, (QT, HEAD)))

    def add_slice(b, n, rows):
        acc[:rows] += jnp.dot(
            x_all[n, :rows],
            w_all[b, pl.ds(pl.multiple_of(n * FEATS, FEATS), FEATS), :],
            preferred_element_type=F32,
        )

    def project(b, rows):
        acc[...] = jnp.zeros_like(acc)

        @pl.loop(0, 8)
        def _(n):
            add_slice(b, n, rows)

    mine, facing = lax.div(z, 4), 1 - lax.div(z, 4)

    def last_slices(*places):
        for dy, half in places:
            add_slice(BLOCKS - 1, lax.rem(y + dy + NY, NY) * 2 + half, BLK)

    def last_first():
        acc[...] = jnp.zeros_like(acc)
        last_slices((0, mine), (0, facing), (1, mine), (-1, mine))

    def last_second():
        last_slices((1, facing), (-1, facing), (2, mine))

    def last_third():
        last_slices((2, facing))
        for hh in range(2):
            keep_block(6 + hh, hh * HEAD)

    def rotate(first, count, lane):
        u = acc[first : first + count, lane : lane + HEAD]
        turned = u * cos_s[first : first + count] + pltpu.roll(u, HEAD // 2, 1) * sin_s[first : first + count]
        return turned.astype(BF16)

    def project_kv():
        project(0, ROWS)
        kv[:, :HEAD] = rotate(0, ROWS, 0)
        kv[:, HEAD:] = acc[:, HEAD:].astype(BF16)

    def keep_block(head, lane):
        q_s[head] = rotate(0, BLK, lane)

    def project_pair(pair):
        project(pair + 1, ROWS if pair < 2 else BLK)
        for hh in range(2):
            head = pair * 2 + hh
            keep_block(head, hh * HEAD)
            if pair < 2:
                qq_s[head * QT : (head + 1) * QT, :] = rotate(BLK, QT, hh * HEAD)

    def others(act):
        @pl.loop(1, N_CTX)
        def _(d):
            act(lax.rem(c + d, N_CTX))

    def own_rows(n):
        return pl.ds(pl.multiple_of(n * OWN, OWN), OWN)

    def exchange(source, target, kind, peer):
        return pltpu.make_async_remote_copy(
            src_ref=source, dst_ref=target, send_sem=ex_send.at[kind], recv_sem=ex_recv.at[kind],
            device_id=(peer, t), device_id_type=MESH,
        )

    def early_rows():
        return own_rows(N_CTX // 2 + lax.div(c, 2))

    def term_to(n):
        return exchange(terms.at[own_rows(lax.div(n, 2))], term_in.at[c], 0, n)

    def qq_to(n):
        return exchange(qq_s.at[early_rows()], qq_s.at[early_rows()], 1, n)

    def mixed_to(n):
        return exchange(mixed_out.at[n], mixed_in.at[c], 2, n)

    def level_to(n):
        return exchange(level_out.at[n], level_in.at[c], 3, n)

    def result_to(n):
        return exchange(result_at(c), result_at(c), 4, n)

    def of_all(kind):
        most = pl.ds(0, N_CTX - 1)
        rows = pl.ds(0, (N_CTX - 1) * OWN)
        piece = (term_in.at[most], qq_s.at[rows], mixed_in.at[most], level_in.at[most], qq_s.at[rows])[kind]
        return exchange(piece, piece, kind, ctx_at(1, 0))

    def query_terms():
        share = x_all[lax.div(c, 4), BLK:, pl.ds(pl.multiple_of(lax.rem(c, 4) * SHARD, SHARD), SHARD)]
        for pair in (2, 3):
            term = jnp.dot(share, w_all[pair + 1, own, :], preferred_element_type=F32)
            first = (pair - 2) * 2 * QT
            terms[first : first + QT, :] = term[:, :HEAD]
            terms[first + QT : first + 2 * QT, :] = term[:, HEAD:]

        @pl.when(lax.rem(c, 2) == 0)
        def _():
            term_in[c] = terms[own_rows(lax.div(c, 2)), :]

        @pl.loop(0, N_CTX // 2)
        def _(d):
            n = 2 * lax.rem(lax.div(c, 2) + d, N_CTX // 2)

            @pl.when(n != c)
            def _():
                term_to(n).start()

    def query_sum():
        @pl.when(lax.rem(c, 2) == 0)
        def _():
            of_all(0).wait_recv()
            u = jnp.sum(term_in[...], 0)
            first = BLK + lax.rem(lax.div(c, 2), QT // OWN) * OWN
            place = pl.ds(pl.multiple_of(first, OWN), OWN)
            turned = u * cos_s[place, :] + pltpu.roll(u, HEAD // 2, 1) * sin_s[place, :]
            qq_s[early_rows(), :] = turned.astype(BF16)
            others(lambda n: qq_to(n).start())

    def by_parity(kind, even, odd, act):
        buffer = term_in if kind == 0 else qq_s
        for parity, count in ((0, even), (1, odd)):
            if count:

                @pl.when(lax.rem(c, 2) == parity)
                def _():
                    piece = buffer.at[pl.ds(0, count if kind == 0 else count * OWN)]
                    act(exchange(piece, piece, kind, ctx_at(1, 0)))

    def query_part():
        by_parity(1, N_CTX // 2 - 1, N_CTX // 2, lambda copy: copy.wait_recv())
        bound = column(bound_ref[...].astype(F32))
        bound = jnp.concatenate([bound] * 2, 0)

        @pl.loop(0, 4)
        def _(pair):
            rows = pl.ds(pl.multiple_of(pair * 2 * QT, 2 * QT), 2 * QT)
            scores = dot_nt(qq_s[rows, :], kv[:BLK, :HEAD])
            place = (lax.broadcasted_iota(jnp.int32, scores.shape, 1) + c * BLK).astype(F32)
            scores = jnp.where(place < bound, scores, NEG)
            peak = jnp.max(scores, 1, keepdims=True)
            weights = jnp.exp2((scores - peak) * POWER)
            total = jnp.sum(weights, 1, keepdims=True)
            mixed = jnp.dot(weights.astype(BF16), kv[:BLK, HEAD:], preferred_element_type=F32)
            for n in range(8):
                mixed_out[pair * 8 + n] = mixed[n * OWN : (n + 1) * OWN].astype(BF16)
            row = lax.broadcasted_iota(jnp.int32, mixed.shape, 0) & (OWN - 1)
            lane = lax.broadcasted_iota(jnp.int32, mixed.shape, 1)
            level = jnp.where(lane == row, peak, jnp.where(lane == row + OWN, total, 0.0))
            level = jnp.sum(level.reshape(8, OWN, HEAD), 1, keepdims=True)
            level_out[pl.ds(pl.multiple_of(pair * 8, 8), 8)] = level

        mixed_in[c] = mixed_out[c]
        level_in[c] = level_out[c]

        def both_to(n):
            mixed_to(n).start()
            level_to(n).start()

        others(both_to)

    def result_at(n):
        return qout_ref.at[
            pl.ds(pl.multiple_of(lax.rem(n, QT // OWN) * OWN, OWN), OWN),
            pl.ds(pl.multiple_of(lax.div(n, QT // OWN) * HEAD, HEAD), HEAD),
        ]

    def query_merge():
        of_all(2).wait_recv()
        of_all(3).wait_recv()

        def levels(first):
            shape = (N_CTX, OWN, HEAD)
            row = lax.broadcasted_iota(jnp.int32, shape, 1)
            lane = lax.broadcasted_iota(jnp.int32, shape, 2)
            kept = jnp.where(lane == row + first, jnp.broadcast_to(level_in[...], shape), 0.0)
            return jnp.sum(kept, 2, keepdims=True)

        peaks = levels(0)
        top = jnp.max(peaks, 0)
        scaled = jnp.exp2((peaks - top[None]) * POWER)
        total_all = jnp.sum(levels(OWN) * scaled, 0)
        mixed_all = jnp.sum(mixed_in[...].astype(F32) * scaled, 0)

        first = lax.rem(c, QT // OWN) * OWN
        scores = dot_nt(qq_s[own_rows(c), :], kv[BLK:, :HEAD])
        row = lax.broadcasted_iota(jnp.int32, scores.shape, 0) + first
        scores = jnp.where(row >= lax.broadcasted_iota(jnp.int32, scores.shape, 1), scores, NEG)
        peak = jnp.max(scores, 1, keepdims=True)
        weights = jnp.exp2((scores - peak) * POWER)
        total = jnp.sum(weights, 1, keepdims=True)
        mixed = jnp.dot(weights.astype(BF16), kv[BLK:, HEAD:], preferred_element_type=F32)
        final = jnp.maximum(top, peak)
        w_ctx = jnp.exp2((top - final) * POWER)
        w_self = jnp.exp2((peak - final) * POWER)
        done = (mixed_all * w_ctx + mixed * w_self) / (total_all * w_ctx + total * w_self)
        result_at(c)[...] = done.astype(BF16)
        others(lambda n: result_to(n).start())

    def attend(head):
        bias = jnp.where(c > 0, 0.0, NEG).astype(F32)
        tile = BLK // 2
        for n in range(2):
            span = (n + 1) * tile
            q = q_s[head, n * tile : span, :]
            far = dot_nt(q, akv[:, :HEAD])
            near = dot_nt(q, kv[:span, :HEAD])
            row = lax.broadcasted_iota(jnp.int32, near.shape, 0) + n * tile
            near = jnp.where(row >= lax.broadcasted_iota(jnp.int32, near.shape, 1), near, NEG)
            peak = jnp.maximum(
                jnp.max(far, 1, keepdims=True) + bias, jnp.max(near, 1, keepdims=True)
            )
            far = jnp.exp2((far - (peak - bias)) * POWER)
            near = jnp.exp2((near - peak) * POWER)
            total = jnp.sum(far, 1, keepdims=True) + jnp.sum(near, 1, keepdims=True)
            mixed = jnp.dot(far.astype(BF16), akv[:, HEAD:], preferred_element_type=F32)
            mixed += jnp.dot(near.astype(BF16), kv[:span, HEAD:], preferred_element_type=F32)
            out_ref[n * tile : span, pl.ds(pl.multiple_of(head * HEAD, HEAD), HEAD)] = (
                mixed / total
            ).astype(BF16)

    def attend_pair(pair):
        @pl.loop(0, 2)
        def _(hh):
            attend(pair * 2 + hh)

    depth = jnp.where(y == 3, 1, y) + jnp.minimum(z, NZ - z)

    def anchor_copy(first, count, target, line, place):
        piece = akv.at[pl.ds(first, count)]
        return pltpu.make_async_remote_copy(
            src_ref=piece, dst_ref=piece, send_sem=a_send.at[line], recv_sem=a_recv.at[place],
            device_id=(target, t), device_id_type=MESH,
        )

    PIECE = BLK // 2
    HALF = BLK // 2

    def anchor_lines(act):
        @pl.when((z == 0) & (y < 2))
        def _():
            act(ctx_at(1, 0), 0)

        @pl.when(c == 0)
        def _():
            act(ctx_at(-1, 0), 1)

        @pl.when(z < 3)
        def _():
            act(ctx_at(0, 1), 2)

        @pl.when((z > 5) | (z == 0))
        def _():
            act(ctx_at(0, -1), 3)

    def anchor_piece(k, target, line):
        return anchor_copy(pl.multiple_of(k * PIECE, PIECE), PIECE, target, line, k)

    def anchor_step(g):
        k = g - depth

        @pl.when((k >= 0) & (k < 2))
        def _():
            @pl.when(depth > 0)
            def _():
                anchor_piece(k, ctx_at(0, 1), 2).wait_recv()

            anchor_lines(lambda target, line: anchor_piece(k, target, line).start())

            @pl.when((z == 3) & (k < 1))
            def _():
                anchor_piece(k, ctx_at(0, 1), 2).start()

            @pl.when((z == 5) & (k >= 1))
            def _():
                anchor_piece(k, ctx_at(0, -1), 3).start()

    def all_angles():
        for n in range(4):
            block_angles(n * (BLK // 4), BLK // 4)
        query_angles()

    def heads(pair):
        return lambda: attend_pair(pair)

    def queries(pair):
        return lambda: project_pair(pair)

    def anchor_root():
        @pl.when(c == 0)
        def _():
            akv[...] = kv[:BLK, :]

    def anchor_end():
        anchor_lines(lambda target, line: anchor_copy(0, BLK, target, line, 0).wait_send())

        @pl.when(z == 3)
        def _():
            anchor_copy(0, HALF, ctx_at(0, 1), 2, 0).wait_send()

        @pl.when(z == 5)
        def _():
            anchor_copy(0, HALF, ctx_at(0, -1), 3, 0).wait_send()

    TASKS = {
        0: (all_angles,),
        2: (x_second,),
        4: (x_third,),
        6: (x_fourth, x_last, project_kv, anchor_root,),
        7: (query_terms,),
        9: (query_sum,),
        10: (queries(0),),
        12: (queries(1),),
        13: (query_part,),
        14: (heads(0),),
        15: (query_merge, queries(2),),
        16: (last_first, heads(1),),
        17: (heads(2), last_second,),
    }

    x_first()

    @pl.loop(0, BLOCKS + LAG)
    def _(i):
        for r in range(STAGGER):
            for s in reversed(range(7)):
                if s % STAGGER == r:
                    b = i - s // STAGGER

                    @pl.when((b >= 0) & (b < BLOCKS))
                    def _():
                        step(b, s)

            anchor_step(STAGGER * i + r - ANCHOR_SLOT)

            for slot, acts in TASKS.items():
                if slot % STAGGER == r:

                    @pl.when(i == slot // STAGGER)
                    def _():
                        for act in acts:
                            act()

    last_third()
    attend(6)
    attend(7)
    of_all(4).wait_recv()

    by_parity(0, N_CTX // 2 - 1, N_CTX // 2, lambda copy: copy.wait_send())
    by_parity(1, N_CTX - 1, 0, lambda copy: copy.wait_send())
    for kind in (2, 3, 4):
        of_all(kind).wait_send()

    @pl.loop(0, BLOCKS)
    def _(b):
        for line in range(4):
            rows = (3 * CUT // 2 + 8 * (3 * REST // 2)) if line < 2 else 7 * REST // 2 + 4 * (7 * CUT // 2)
            w_copy(b, pl.ds(0, rows), ctx_at(1, 0), line, 0).wait_send()

    for way in (0, 1):
        for chunk in range(4):
            x_near(way, chunk, 0).wait_send()
        for chunk in FAR[way]:
            x_far(way, chunk, 0).wait_send()
    for dx in (0, 1, -1, 2):
        x_across(dx).wait_send()
    anchor_end()


def on_device(rows, query_rows, positions, bound, wq, wk, wv):
    freq = np.asarray(rope_table(HEAD // 2) * 2, np.float32)[None]
    anywhere = pl.BlockSpec(memory_space=pl.ANY)
    vmem = pl.BlockSpec(memory_space=pltpu.VMEM)
    dma = pltpu.SemaphoreType.DMA
    return pl.pallas_call(
        kernel,
        out_shape=(
            pltpu.VMEM((BLK, 8 * HEAD), BF16),
            pltpu.VMEM((QT, 8 * HEAD), BF16),
        ),
        in_specs=[anywhere] * 5 + [vmem] * 3,
        out_specs=(vmem, vmem),
        scratch_shapes=[
            pltpu.VMEM((BLOCKS, N_CTX * SHARD, COLS), BF16),
            pltpu.VMEM((8, ROWS, FEATS), BF16),
            pltpu.VMEM((ROWS, HEAD), F32),
            pltpu.VMEM((ROWS, HEAD), F32),
            pltpu.VMEM((ROWS, COLS), F32),
            pltpu.VMEM((ROWS, COLS), BF16),
            pltpu.VMEM((BLK, COLS), BF16),
            pltpu.VMEM((8, BLK, HEAD), BF16),
            pltpu.VMEM((8 * QT, HEAD), BF16),
            pltpu.VMEM((4 * QT, HEAD), F32),
            pltpu.VMEM((N_CTX, OWN, HEAD), F32),
            pltpu.VMEM((N_CTX, OWN, HEAD), BF16),
            pltpu.VMEM((N_CTX, OWN, HEAD), BF16),
            pltpu.VMEM((N_CTX, 1, HEAD), F32),
            pltpu.VMEM((N_CTX, 1, HEAD), F32),
            dma((3 + BLOCKS,)),
            dma((BLOCKS, 4)),
            dma((BLOCKS, PLACES)),
            dma((3, 4)),
            dma((3, 4)),
            dma((4,)),
            dma((4,)),
            dma((4,)),
            dma((4,)),
            dma((5,)),
            dma((5,)),
        ],
        compiler_params=pltpu.CompilerParams(
            collective_id=0, has_side_effects=True, vmem_limit_bytes=56 << 20
        ),
        name="star_prefill",
    )(rows, query_rows, wq, wk, wv, positions[None], bound[None], freq)


def solution(mesh):
    placed = (
        P("ctx", "tp"),
        P(None, "tp"),
        P(),
        P(),
        P("ctx", "tp"),
        P("ctx", "tp"),
        P("ctx", "tp"),
    )
    return jax.shard_map(
        on_device,
        mesh=mesh,
        in_specs=placed,
        out_specs=(P("ctx", "tp"), P(None, "tp")),
        check_vma=False,
    )
```
